256 devices in a mesh: dp: 4 (over x), expert: 64 (over y, z, core).
Axes of the slice: x: 4, y: 4, z: 8, core: 2. Of those that a mesh axis runs over, the one named last changes fastest.
Arguments:
- stash_codes: bfloat16 [32768, 7168], P(('dp', 'expert')), may hold values from -6 to 6
- stash_scales: float32 [32768, 56], P(('dp', 'expert')), may hold values from 0.3 to 3
- expert_ids: int32 [32768, 8], P(('dp', 'expert')), may hold values from 0 to 255, as said below
- grad_rows: bfloat16 [256, 768, 1024], P(('dp', 'expert')), may hold values from -0.119628906 to 0.119628906
Outputs:
- weight_grad: bfloat16 [64, 7168, 1024], P(None, 'expert', 'dp')
The draws below stay inside these ranges and needn't reach their ends.
Inputs may be any that keep to these rules, and one draw needn't show every extreme that they name: `expert_ids`: each row names 8 different experts. In the 128 rows of one device, an expert e with e % 4 == 0 is named by at most 12 rows; for each dp index, one such expert is named by exactly 12 rows on every device of that index.
All inputs are finite; a program needn't handle non-finite values.
Results may differ from the reference program's by a relative error of at most 0.022.
Values may be sent and summed in bfloat16 or wider, within the bound.
A program may use at most 128 MiB of HBM per device.

```python
import math
import jax
import jax.numpy as jnp
from jax import lax

D = 7168
TOPK = 8
QB = 128
HW = 1024
EXP_DEV = 4
TOK_DEV = 128
CAP = 12
EXPERTS = 256
TOKENS = 32768
SLOTS = 768
N_DP = 4
N_EXPERT = 64


def draw_expert_ids(key, part):
    key = jax.random.fold_in(key, 7)
    key_base, key_pop, key_hot, key_off = jax.random.split(key, 4)
    blocks = N_DP * N_EXPERT
    base_draw = jax.random.randint(key_base, (blocks, TOK_DEV, EXPERTS), 0, 2 ** 18)
    expert = jnp.arange(EXPERTS, dtype=jnp.int32)
    flight = expert % EXP_DEV == 0
    pop_flight = jax.random.randint(key_pop, (blocks, EXPERTS), 4, 8)
    pop_other = jax.random.randint(jax.random.fold_in(key_pop, 1), (blocks, EXPERTS), 0, 6)
    popularity = jnp.where(flight[None, :], pop_flight, pop_other)
    scores = base_draw * EXPERTS + expert[None, None, :] + (popularity * (EXPERTS * 2 ** 18))[:, None, :]
    hot_group = jax.random.randint(key_hot, (N_DP,), 0, N_EXPERT)
    hot_owner = jnp.repeat(hot_group, N_EXPERT)
    offset = jax.random.randint(key_off, (blocks, EXPERTS), 0, TOK_DEV)
    position = jnp.arange(TOK_DEV, dtype=jnp.int32)
    inside = (position[None, :, None] - offset[:, None, :]) % TOK_DEV < CAP
    is_hot = expert[None, :] == (hot_owner * EXP_DEV)[:, None]
    allowed = jnp.where(flight[None, None, :], inside, True)
    forced = is_hot[:, None, :] & inside
    scores = jnp.where(forced, scores + 2 ** 30, scores)
    scores = jnp.where(allowed, scores, -1 - expert[None, None, :])
    _, chosen = lax.top_k(scores, TOPK)
    return chosen.reshape(blocks * TOK_DEV, TOPK).astype(jnp.int32)


def block_scale(stream_key, extent, cuts, smallest, top_value):
    level, own = 1.0, jax.random.fold_in(stream_key, 6)
    for dim, blocks in cuts:
        steps = jnp.exp(jax.random.uniform(jax.random.fold_in(own, dim), (blocks,), jnp.float32, smallest / len(cuts), top_value / len(cuts)))
        level = level * jnp.repeat(steps, extent[dim] // blocks).reshape([-1 if axis == dim else 1 for axis in range(len(extent))])
    return level


def scatter_about(key, extent, deviation, most, pieces=(), kind=jnp.bfloat16):
    result = jax.random.normal(key, extent, jnp.float32) * deviation
    if len(pieces) > 0:
        result = block_scale(key, extent, pieces, -0.22, 0.18) * result
    return jnp.clip(result, min=-most, max=most).astype(kind)


def setup_inputs(seed: int = 0) -> dict:
    keys = jax.random.split(jax.random.key(seed), 5)
    return {
        "stash_codes": scatter_about(keys[0], (TOKENS, D), 1.0, 6.0, ((0, 256),)),
        "stash_scales": jnp.clip(jnp.exp(math.log(3.0) - 2.3025851 * jax.random.uniform(keys[1], (TOKENS, D // QB), jnp.float32) ** block_scale(keys[1], (TOKENS, D // QB), ((0, 256),), -0.2, 0.2)), 0.3, 3.0),
        "expert_ids": draw_expert_ids(jax.random.fold_in(keys[4], 71), 0),
        "grad_rows": scatter_about(keys[3], (N_DP * N_EXPERT, SLOTS, HW), 0.02, 0.119628906, ((0, 256),)),
    }


def hadamard(order):
    row_bits = jnp.arange(order, dtype=jnp.int32)[:, None]
    col_bits = jnp.arange(order, dtype=jnp.int32)[None, :]
    common = jnp.bitwise_and(row_bits, col_bits)
    parity = jnp.zeros((order, order), jnp.int32)
    for bit in range(order.bit_length() - 1):
        parity = parity + jnp.bitwise_and(jnp.right_shift(common, bit), 1)
    return (1 - 2 * (parity % 2)).astype(jnp.bfloat16)

def restore(codes, scales):
    row_count = codes.shape[0]
    block_count = codes.shape[1] // QB
    dequant = (codes.astype(jnp.float32).reshape(row_count, block_count, QB) * scales[:, :, None]).astype(jnp.bfloat16)
    turned = jnp.dot(dequant.reshape(row_count * block_count, QB), hadamard(QB), preferred_element_type=jnp.float32)
    return (turned * QB ** (-0.5)).astype(jnp.bfloat16).reshape(row_count, block_count * QB)

def slot_tables(routes, owners):
    targets = jnp.arange(owners, dtype=jnp.int32) * EXP_DEV
    member = jnp.any(routes[:, :, None] == targets[None, None, :], axis=1).astype(jnp.int32)
    ranking = jnp.cumsum(member, axis=0) - member
    slot_index = jnp.arange(CAP, dtype=jnp.int32)
    selector = member.T[:, None, :] * (ranking.T[:, None, :] == slot_index[None, :, None]).astype(jnp.int32)
    positions = jnp.arange(routes.shape[0], dtype=jnp.int32)
    source = lax.optimization_barrier(jnp.sum(selector * positions[None, None, :], axis=2)).astype(jnp.int32)
    filled = lax.optimization_barrier(jnp.sum(selector, axis=2)).astype(jnp.int32)
    return (source, filled)

def reference(stash_codes, stash_scales, expert_ids, grad_rows):
    blocks = N_DP * N_EXPERT
    codes_blocks = stash_codes.reshape(blocks, TOK_DEV, D)
    scale_blocks = stash_scales.reshape(blocks, TOK_DEV, D // QB)
    restored = lax.map(lambda pair: restore(pair[0], pair[1]), (codes_blocks, scale_blocks))
    source, filled = jax.vmap(lambda routes: slot_tables(routes, N_EXPERT))(expert_ids.reshape(blocks, TOK_DEV, TOPK))
    senders = jnp.arange(N_EXPERT, dtype=jnp.int32)[:, None]

    def owner_grad(owner):
        running = jnp.zeros((HW, D), jnp.float32)
        for group in range(N_DP):
            first_block = group * N_EXPERT
            chosen_rows = lax.dynamic_index_in_dim(source[first_block:first_block + N_EXPERT], owner, 1, keepdims=False)
            slot_filled = lax.dynamic_index_in_dim(filled[first_block:first_block + N_EXPERT], owner, 1, keepdims=False)
            gathered = restored[first_block + senders, chosen_rows]
            gathered = gathered * slot_filled[:, :, None].astype(jnp.bfloat16)
            gradient = lax.dynamic_index_in_dim(grad_rows, first_block + owner, 0, keepdims=False)
            partial_value = jnp.dot(gradient.T, gathered.reshape(N_EXPERT * CAP, D), preferred_element_type=jnp.float32).astype(jnp.bfloat16)
            running = running + lax.optimization_barrier(partial_value).astype(jnp.float32)
        return running.T.astype(jnp.bfloat16)
    return lax.map(owner_grad, jnp.arange(N_EXPERT, dtype=jnp.int32))
```

```python
import jax
import jax.numpy as jnp
from jax import lax
from jax.experimental import pallas as pl
from jax.experimental.pallas import tpu as pltpu
from jax.sharding import PartitionSpec as P

QB = 128
EXP_DEV = 4
CAP = 12
D = 7168
HW = 1024
TOK = 128
NX, NY, NZ = 4, 4, 8
RING = 2 * NZ
OWNERS = NY * RING
COLS = D // OWNERS
WIDTH = NY * COLS
SLOTS = OWNERS * CAP
HSH = HW // NX
TAB = 32
QUAD = 4
MESH = pl.DeviceIdType.MESH
BF16 = jnp.bfloat16
F32 = jnp.float32


def slot_table(routes):
    targets = jnp.arange(OWNERS, dtype=jnp.int32) * EXP_DEV
    member = jnp.any(routes[:, :, None] == targets[None, None, :], axis=1).astype(jnp.int32)
    ranking = jnp.cumsum(member, axis=0) - member
    slot_index = jnp.arange(CAP, dtype=jnp.int32)
    selector = member.T[:, None, :] * (ranking.T[:, None, :] == slot_index[None, :, None]).astype(
        jnp.int32
    )
    positions = jnp.arange(routes.shape[0], dtype=jnp.int32)
    token = jnp.sum(selector * (positions[None, None, :] + 1), axis=2) - 1
    token = token.reshape(NY, RING, 1, CAP)
    place = lax.axis_index("expert") % QUAD
    mine = (jnp.arange(QUAD, dtype=jnp.int32) == place)[None, None, :, None]
    spread = jnp.where(mine, token, -1).reshape(NY, RING * QUAD * CAP // 128, 128)
    spread = jnp.pad(spread, ((0, 0), (0, TAB // NY - spread.shape[1]), (0, 0)), constant_values=-1)
    return spread.reshape(TAB, 128).astype(BF16)


def rem(value, count):
    return lax.rem(value + count, count)


def kernel(
    codes, scales, table, grad, out, gbuf,
    send, tok, onehot, rows, gv, part, r1, r2, total,
    zs, zr, ys, yr, yfs, yfr, gs, gr, ss, sr, gl,
    s1s, s1r, s2s, s2r, cs, cr, cl, ol,
):
    x = lax.axis_index("dp")
    me = lax.axis_index("expert")
    y = lax.div(me, RING)
    zc = lax.rem(me, RING)
    z = lax.div(zc, 2)
    c = lax.rem(zc, 2)
    own = zc
    up_x, down_x = rem(x + 1, NX), rem(x - 1, NX)
    up_y, down_y = rem(y + 1, NY), rem(y - 1, NY)
    far_y = rem(y + 2, NY)
    up_z, down_z = rem(z + 1, NZ), rem(z - 1, NZ)
    dev_up_z = y * RING + 2 * up_z + c
    dev_down_z = y * RING + 2 * down_z + c
    sibling = y * RING + 2 * z + (1 - c)

    def rdma(src, dst, send_sem, recv_sem, dev_x, dev_e):
        return pltpu.make_async_remote_copy(
            src_ref=src, dst_ref=dst, send_sem=send_sem, recv_sem=recv_sem,
            device_id=(dev_x, dev_e), device_id_type=MESH,
        )

    barrier = pltpu.get_barrier_semaphore()
    for k in range(1, RING):
        pl.semaphore_signal(barrier, inc=1, device_id=(x, y * RING + rem(zc + k, RING)), device_id_type=MESH)
    for k in range(1, NY):
        pl.semaphore_signal(barrier, inc=1, device_id=(x, rem(y + k, NY) * RING + zc), device_id_type=MESH)
    for dev_x in (up_x, down_x):
        pl.semaphore_signal(barrier, inc=1, device_id=(dev_x, me), device_id_type=MESH)

    row_id = lax.broadcasted_iota(jnp.int32, (QB, QB), 0)
    col_id = lax.broadcasted_iota(jnp.int32, (QB, QB), 1)
    common = row_id & col_id
    parity = jnp.zeros((QB, QB), jnp.int32)
    for bit in range(7):
        parity = parity + ((common >> bit) & 1)
    had = (1 - 2 * (parity & 1)).astype(F32).astype(BF16)
    for k in range(D // QB):
        deq = (codes[:, k * QB:(k + 1) * QB].astype(F32) * scales[:, k:k + 1]).astype(BF16)
        turned = lax.dot_general(had, deq, (((1,), (1,)), ((), ())), preferred_element_type=F32)
        turned = (turned * QB ** (-0.5)).astype(BF16)
        start = 0
        while start < QB:
            n = k * QB + start
            idx, off = n // COLS, n % COLS
            length = min(QB - start, COLS - off)
            ty, tz = idx // RING, idx % RING
            send[tz, ty * COLS + off:ty * COLS + off + length, :] = turned[start:start + length]
            start += length
    for k in range(RING):
        send[k, WIDTH:WIDTH + TAB, :] = table[...]

    pl.semaphore_wait(barrier, RING - 1 + NY - 1 + 2)

    def z_copy(k, target, source):
        return rdma(
            send.at[target], tok.at[y * RING + source], zs.at[k], zr.at[k], x, y * RING + target
        )

    own_copy = pltpu.make_async_copy(send.at[own], tok.at[me], ol.at[0])
    own_copy.start()
    order = sorted(range(1, RING), key=lambda k: (min(k, RING - k), k))
    for k in order:
        z_copy(k, rem(zc + k, RING), zc).start()

    first_load = pltpu.make_async_copy(grad.at[0], gv.at[0], gl.at[0])
    first_load.start()

    def ring_z(j):
        return rem(z + (j + 1) // 2, NZ) if j % 2 else rem(z - j // 2, NZ)

    def piece(ref, j):
        if j == 7:
            return ref.at[pl.ds(SLOTS // 2, SLOTS // 2)]
        if j == 8:
            return ref.at[pl.ds(0, SLOTS // 2)]
        return ref

    def ring_copy(j, src, index):
        target = dev_down_z if j % 2 else dev_up_z
        return rdma(piece(src, j), piece(gbuf.at[index], j), gs.at[j], gr.at[j], x, target)

    def pair_copy(j, src, index):
        return rdma(piece(src, j), piece(gbuf.at[index], j), ss.at[j], sr.at[j], x, sibling)

    ring_copy(1, grad.at[0], own).start()
    ring_copy(2, grad.at[0], own).start()
    pair_copy(0, grad.at[0], own).start()

    def ring_step(j):
        index = 2 * ring_z(j) + c
        ring_copy(j, gbuf.at[index], index).wait_recv()
        if j <= 6:
            ring_copy(j + 2, gbuf.at[index], index).start()
        pair_copy(j, gbuf.at[index], index).start()

    def chunk(group, j):
        return tok.at[pl.ds(group * RING + 2 * ring_z(j), 2)]

    def y_copy(way, j, group, target):
        ref = chunk(group, j)
        return rdma(ref, ref, ys.at[way, j], yr.at[way, j], x, target * RING + zc)

    def far_copy(j, group):
        ref = chunk(group, j)
        target = down_y if j % 2 else up_y
        return rdma(ref, ref, yfs.at[j], yfr.at[j], x, target * RING + zc)

    for j in range(NZ):
        if j == 0:
            own_copy.wait()
            source = 2 * z + (1 - c)
            k = rem(zc - source, RING)
            z_copy(k, source, source).wait_recv()
        else:
            for core in range(2):
                source = 2 * ring_z(j) + core
                k = rem(zc - source, RING)
                z_copy(k, source, source).wait_recv()
        y_copy(0, j, y, up_y).start()
        y_copy(1, j, y, down_y).start()
    for j in range(NZ):
        y_copy(0, j, down_y, up_y).wait_recv()
        y_copy(1, j, up_y, down_y).wait_recv()
        far_copy(j, up_y if j % 2 else down_y).start()

    lane = lax.broadcasted_iota(jnp.int32, (128, 128), 1).astype(F32)

    def gather(q):
        for p in range(QUAD):
            words = tok[QUAD * q + p, WIDTH:WIDTH + TAB, :].astype(F32)
            each = TAB // NY
            mine = words[0:each]
            for group in range(1, NY):
                mine = jnp.where(y == group, words[group * each:(group + 1) * each], mine)
            for part_id in range(RING * QUAD * CAP // 128):
                column = jnp.broadcast_to(mine[part_id:part_id + 1, :], (128, 128)).T
                onehot[part_id * 128:(part_id + 1) * 128, p * 128:(p + 1) * 128] = jnp.where(
                    column == lane, 1.0, 0.0
                ).astype(BF16)
        blocks = jnp.concatenate([tok[QUAD * q + p, 0:WIDTH, :] for p in range(QUAD)], axis=1)
        picked = lax.dot_general(
            onehot[...], blocks, (((1,), (1,)), ((), ())), preferred_element_type=F32
        ).astype(BF16)
        height = QUAD * CAP
        for e in range(RING):
            rows[e, pl.ds(pl.multiple_of(q * height, height), height), :] = picked[
                e * height:(e + 1) * height
            ]

    quads = RING // QUAD

    def gather_step(step, carry):
        group = rem(y + lax.div(step, quads) - 1, NY)
        gather(group * quads + lax.rem(step, quads))
        return carry

    lax.fori_loop(0, 3 * quads, gather_step, 0)
    ring_step(1)
    ring_step(2)
    for j in range(NZ):
        far_copy(j, far_y).wait_recv()
    lax.fori_loop(3 * quads, 4 * quads, gather_step, 0)

    def place(i):
        j = lax.div(i, 2)
        half = lax.div(j + 1, 2)
        zj = rem(jnp.where(lax.rem(j, 2) == 1, z + half, z - half + NZ), NZ)
        core = rem(c + lax.rem(i, 2), 2)
        return 2 * zj + core

    def load(i):
        return pltpu.make_async_copy(gbuf.at[place(i)], gv.at[lax.rem(i, 2)], gl.at[lax.rem(i, 2)])

    half_rows = WIDTH // 2
    top, bottom = pl.ds(0, half_rows), pl.ds(half_rows, half_rows)
    opposite = rem(x + 2, NX)

    def first_copies(i):
        slot = lax.rem(i, 3)
        return (
            rdma(part.at[slot, opposite, top], r1.at[i, 0], s1s.at[i, 0], s1r.at[i, 0], up_x, me),
            rdma(part.at[slot, opposite, bottom], r1.at[i, 1], s1s.at[i, 1], s1r.at[i, 1], down_x, me),
        )

    def second_copies(i):
        slot = lax.rem(i, 3)
        return (
            rdma(part.at[slot, up_x], r2.at[i, 0], s2s.at[i, 0], s2r.at[i, 0], up_x, me),
            rdma(part.at[slot, down_x], r2.at[i, 1], s2s.at[i, 1], s2r.at[i, 1], down_x, me),
        )

    def out_copies(i):
        slot = lax.rem(i, 2)
        copies = []
        for k in range(1, NY):
            target = rem(y + k, NY)
            copies.append(rdma(
                total.at[slot, target], out.at[y * RING + place(i)],
                cs.at[i, k - 1], cr.at[i, k - 1], x, target * RING + zc,
            ))
        return copies

    def arrivals(i):
        slot = lax.rem(i, 2)
        return [
            rdma(
                total.at[slot, rem(y + k, NY)], out.at[rem(y - k, NY) * RING + place(i)],
                cs.at[i, k - 1], cr.at[i, k - 1], x, rem(y + k, NY) * RING + zc,
            )
            for k in range(1, NY)
        ]

    def own_out(i):
        slot = lax.rem(i, 2)
        return pltpu.make_async_copy(total.at[slot, y], out.at[y * RING + place(i)], cl.at[slot])

    def sent(i):
        for copy in first_copies(i):
            copy.wait_send()
        for copy in second_copies(i):
            copy.wait_send()

    def given(i):
        for copy in out_copies(i):
            copy.wait_send()
        own_out(i).wait()

    def main_step(i, carry):
        for at in (4, 8, 12):
            @pl.when(i == at)
            def _():
                ring_step(at // 2 + 1)
                ring_step(at // 2 + 2)

        @pl.when(i + 1 < RING)
        def _():
            j = lax.div(i + 1, 2)
            index = place(i + 1)

            @pl.when(jnp.logical_and(lax.rem(i, 2) == 0, j < NZ - 1))
            def _():
                rdma(gbuf.at[index], gbuf.at[index], ss.at[j], sr.at[j], x, sibling).wait_recv()

            @pl.when(jnp.logical_and(lax.rem(i, 2) == 0, j == NZ - 1))
            def _():
                for k in (7, 8):
                    pair_copy(k, gbuf.at[index], index).wait_recv()

            load(i + 1).start()

        @pl.when(i < RING)
        def _():
            slot, held = lax.rem(i, 3), lax.rem(i, 2)

            @pl.when(i >= 3)
            def _():
                sent(i - 3)

            pltpu.make_async_copy(grad.at[0], gv.at[held], gl.at[held]).wait()
            expert = place(i)
            for t in range(NX):
                part[slot, t] = lax.dot_general(
                    rows[expert], gv[held, :, t * HSH:(t + 1) * HSH],
                    (((0,), (0,)), ((), ())), preferred_element_type=F32,
                ).astype(BF16)
            for copy in first_copies(i):
                copy.start()

        @pl.when(jnp.logical_and(i >= 1, i < RING + 1))
        def _():
            b = i - 1
            slot = lax.rem(b, 3)
            for copy in first_copies(b):
                copy.wait_recv()
            part[slot, up_x, top] = (
                part[slot, up_x, top].astype(F32) + r1[b, 0].astype(F32)
            ).astype(BF16)
            part[slot, down_x, bottom] = (
                part[slot, down_x, bottom].astype(F32) + r1[b, 1].astype(F32)
            ).astype(BF16)
            for copy in second_copies(b):
                copy.start()

        @pl.when(i >= 2)
        def _():
            b = i - 2
            slot = lax.rem(b, 3)

            @pl.when(b >= 2)
            def _():
                given(b - 2)

            for copy in second_copies(b):
                copy.wait_recv()
            for group in range(NY):
                cut = pl.ds(group * COLS, COLS)
                total[lax.rem(b, 2), group] = (
                    part[slot, x, cut].astype(F32)
                    + r2[b, 0, cut].astype(F32)
                    + r2[b, 1, cut].astype(F32)
                ).astype(BF16)
            for copy in out_copies(b):
                copy.start()
            own_out(b).start()

        return carry

    lax.fori_loop(0, RING + 2, main_step, 0)

    def close(i, carry):
        for copy in arrivals(i):
            copy.wait_recv()
        return carry

    lax.fori_loop(0, RING, close, 0)
    for i in range(RING - 3, RING):
        sent(jnp.int32(i))
    for i in range(RING - 2, RING):
        given(jnp.int32(i))
    for k in range(1, RING):
        z_copy(k, rem(zc + k, RING), zc).wait_send()
    for j in range(NZ):
        y_copy(0, j, y, up_y).wait_send()
        y_copy(1, j, y, down_y).wait_send()
        far_copy(j, up_y if j % 2 else down_y).wait_send()
    for j in range(1, 9):
        ring_copy(j, grad.at[0], own).wait_send()
    for j in range(0, 9):
        pair_copy(j, grad.at[0], own).wait_send()


def local(stash_codes, stash_scales, expert_ids, grad_rows):
    table = slot_table(expert_ids)
    vmem = pl.BlockSpec(memory_space=pltpu.VMEM)
    hbm = pl.BlockSpec(memory_space=pl.ANY)
    dma = pltpu.SemaphoreType.DMA
    weight_grad, _ = pl.pallas_call(
        kernel,
        out_shape=(
            jax.ShapeDtypeStruct((OWNERS, COLS, HSH), BF16),
            jax.ShapeDtypeStruct((RING, SLOTS, HW), BF16),
        ),
        in_specs=[vmem, vmem, vmem, hbm],
        out_specs=(hbm, hbm),
        scratch_shapes=[
            pltpu.VMEM((RING, WIDTH + TAB, TOK), BF16),
            pltpu.VMEM((OWNERS, WIDTH + TAB, TOK), BF16),
            pltpu.VMEM((RING * QUAD * CAP, QUAD * TOK), BF16),
            pltpu.VMEM((RING, SLOTS, WIDTH), BF16),
            pltpu.VMEM((2, SLOTS, HW), BF16),
            pltpu.VMEM((3, NX, WIDTH, HSH), BF16),
            pltpu.VMEM((RING, 2, WIDTH // 2, HSH), BF16),
            pltpu.VMEM((RING, 2, WIDTH, HSH), BF16),
            pltpu.VMEM((2, NY, COLS, HSH), BF16),
            dma((RING,)), dma((RING,)),
            dma((2, NZ)), dma((2, NZ)), dma((NZ,)), dma((NZ,)),
            dma((9,)), dma((9,)), dma((9,)), dma((9,)), dma((2,)),
            dma((RING, 2)), dma((RING, 2)), dma((RING, 2)), dma((RING, 2)),
            dma((RING, 3)), dma((RING, 3)), dma((2,)), dma((1,)),
        ],
        compiler_params=pltpu.CompilerParams(
            collective_id=0, has_side_effects=True, vmem_limit_bytes=58 * 1024 * 1024
        ),
        cost_estimate=pl.CostEstimate(
            flops=2 * SLOTS * D * HW, bytes_accessed=100_000_000, transcendentals=0
        ),
    )(stash_codes, stash_scales, table, grad_rows)
    return weight_grad


def solution(mesh):
    return jax.shard_map(
        local,
        mesh=mesh,
        in_specs=(
            P(("dp", "expert"), None),
            P(("dp", "expert"), None),
            P(("dp", "expert"), None),
            P(("dp", "expert"), None, None),
        ),
        out_specs=P(None, "expert", "dp"),
        check_vma=False,
    )
```

```python
import jax
import jax.numpy as jnp
from jax import lax
from jax.experimental import pallas as pl
from jax.experimental.pallas import tpu as pltpu
from jax.sharding import PartitionSpec as P

QB = 128
EXP_DEV = 4
CAP = 12
D = 7168
HW = 1024
TOK = 128
NX, NY, NZ = 4, 4, 8
RING = 2 * NZ
OWNERS = NY * RING
COLS = D // OWNERS
WIDTH = NY * COLS
SLOTS = OWNERS * CAP
HSH = HW // NX
TAB = 32
HALVES = 2
PART = WIDTH // HALVES
UNITS = RING * HALVES
DEPTH = 6
KEEP = 4
CUTS = 4
QUAD = 4
MESH = pl.DeviceIdType.MESH
BF16 = jnp.bfloat16
F32 = jnp.float32


def slot_table(routes):
    targets = jnp.arange(OWNERS, dtype=jnp.int32) * EXP_DEV
    member = jnp.any(routes[:, :, None] == targets[None, None, :], axis=1).astype(jnp.int32)
    ranking = jnp.cumsum(member, axis=0) - member
    slot_index = jnp.arange(CAP, dtype=jnp.int32)
    selector = member.T[:, None, :] * (ranking.T[:, None, :] == slot_index[None, :, None]).astype(
        jnp.int32
    )
    positions = jnp.arange(routes.shape[0], dtype=jnp.int32)
    token = jnp.sum(selector * (positions[None, None, :] + 1), axis=2) - 1
    token = token.reshape(NY, RING, 1, CAP)
    place = lax.axis_index("expert") % QUAD
    mine = (jnp.arange(QUAD, dtype=jnp.int32) == place)[None, None, :, None]
    spread = jnp.where(mine, token, -1).reshape(NY, RING * QUAD * CAP // 128, 128)
    spread = jnp.pad(spread, ((0, 0), (0, TAB // NY - spread.shape[1]), (0, 0)), constant_values=-1)
    return spread.reshape(TAB, 128).astype(BF16)


def rem(value, count):
    return lax.rem(value + count, count)


def kernel(
    codes, scales, table, grad, out, gbuf,
    code, send0, send1, tok0, tok1, onehot, rows, gv, part, r1, r2, total,
    il, ol, zs, zr, ys, yr, yfs, yfr, gs, gr, ss, sr, gl,
    s1s, s1r, s2s, s2r, cs, cr, cl,
):
    x = lax.axis_index("dp")
    me = lax.axis_index("expert")
    y = lax.div(me, RING)
    zc = lax.rem(me, RING)
    z = lax.div(zc, 2)
    c = lax.rem(zc, 2)
    own = zc
    up_x, down_x = rem(x + 1, NX), rem(x - 1, NX)
    up_y, down_y = rem(y + 1, NY), rem(y - 1, NY)
    far_y = rem(y + 2, NY)
    dev_up_z = y * RING + 2 * rem(z + 1, NZ) + c
    dev_down_z = y * RING + 2 * rem(z - 1, NZ) + c
    sibling = y * RING + 2 * z + (1 - c)
    send, tok = (send0, send1), (tok0, tok1)

    def rdma(src, dst, send_sem, recv_sem, dev_x, dev_e):
        return pltpu.make_async_remote_copy(
            src_ref=src, dst_ref=dst, send_sem=send_sem, recv_sem=recv_sem,
            device_id=(dev_x, dev_e), device_id_type=MESH,
        )

    step = D // CUTS
    fetches = [
        pltpu.make_async_copy(
            codes.at[:, pl.ds(k * step, step)], code.at[:, pl.ds(k * step, step)], il.at[k]
        )
        for k in range(CUTS)
    ]
    for fetch in fetches:
        fetch.start()

    barrier = pltpu.get_barrier_semaphore()
    for k in range(1, RING):
        pl.semaphore_signal(barrier, inc=1, device_id=(x, y * RING + rem(zc + k, RING)), device_id_type=MESH)
    for k in range(1, NY):
        pl.semaphore_signal(barrier, inc=1, device_id=(x, rem(y + k, NY) * RING + zc), device_id_type=MESH)
    for dev_x in (up_x, down_x):
        pl.semaphore_signal(barrier, inc=1, device_id=(dev_x, me), device_id_type=MESH)

    row_id = lax.broadcasted_iota(jnp.int32, (QB, QB), 0)
    col_id = lax.broadcasted_iota(jnp.int32, (QB, QB), 1)
    common = row_id & col_id
    parity = jnp.zeros((QB, QB), jnp.int32)
    for bit in range(7):
        parity = parity + ((common >> bit) & 1)
    had = (1 - 2 * (parity & 1)).astype(F32).astype(BF16)

    def restore(half):
        blocks = D // QB // HALVES
        for k in range(half * blocks, (half + 1) * blocks):
            if k % (D // QB // CUTS) == 0:
                fetches[k // (D // QB // CUTS)].wait()
            turned = lax.dot_general(
                had, code[:, k * QB:(k + 1) * QB], (((1,), (1,)), ((), ())), preferred_element_type=F32
            )
            turned = (turned * (scales[k:k + 1, :] * QB ** (-0.5))).astype(BF16)
            start = 0
            while start < QB:
                n = k * QB + start
                idx, off = n // COLS, n % COLS
                length = min(QB - start, COLS - off)
                ty, tz = idx // RING, idx % RING
                at = (ty - half * (NY // HALVES)) * COLS + off
                send[half][tz, at:at + length, :] = turned[start:start + length]
                start += length

    def z_copy(half, k, target, source):
        return rdma(
            send[half].at[target], tok[half].at[y * RING + source],
            zs.at[half, k], zr.at[half, k], x, y * RING + target,
        )

    own_copies = [
        pltpu.make_async_copy(send[half].at[own], tok[half].at[me], ol.at[half]) for half in range(HALVES)
    ]
    order = sorted(range(1, RING), key=lambda k: (min(k, RING - k), k))
    for k in range(RING):
        send0[k, PART:PART + TAB, :] = table[...]
    for half in range(HALVES):
        restore(half)
        if half == 0:
            pl.semaphore_wait(barrier, RING - 1 + NY - 1 + 2)
        for k in order:
            z_copy(half, k, rem(zc + k, RING), zc).start()
        own_copies[half].start()

    first_load = pltpu.make_async_copy(grad.at[0], gv.at[0], gl.at[0])
    first_load.start()

    def ring_z(j):
        return rem(z + (j + 1) // 2, NZ) if j % 2 else rem(z - j // 2, NZ)

    def cut(ref, h):
        return ref.at[pl.ds(h * (SLOTS // 2), SLOTS // 2)]

    def ring_copy(j, h, src, index):
        target = dev_down_z if j % 2 else dev_up_z
        return rdma(cut(src, h), cut(gbuf.at[index], h), gs.at[j, h], gr.at[j, h], x, target)

    def pair_copy(j, h, src, index):
        return rdma(cut(src, h), cut(gbuf.at[index], h), ss.at[j, h], sr.at[j, h], x, sibling)

    def holds(j, h):
        return not (j == 7 and h == 0 or j == 8 and h == 1)

    for h in range(2):
        ring_copy(1, h, grad.at[0], own).start()
        ring_copy(2, h, grad.at[0], own).start()
        pair_copy(0, h, grad.at[0], own).start()

    def ring_step(distance, h):
        for j in (2 * distance - 1, 2 * distance):
            if holds(j, h):
                index = 2 * ring_z(j) + c
                ring_copy(j, h, gbuf.at[index], index).wait_recv()
                if j <= 6 and holds(j + 2, h):
                    ring_copy(j + 2, h, gbuf.at[index], index).start()
                pair_copy(j, h, gbuf.at[index], index).start()

    def chunk(half, group, j):
        return tok[half].at[pl.ds(group * RING + 2 * ring_z(j), 2)]

    def y_copy(half, way, j, group, target):
        ref = chunk(half, group, j)
        return rdma(ref, ref, ys.at[half, way, j], yr.at[half, way, j], x, target * RING + zc)

    def far_copy(half, j, group):
        ref = chunk(half, group, j)
        target = down_y if j % 2 else up_y
        return rdma(ref, ref, yfs.at[half, j], yfr.at[half, j], x, target * RING + zc)

    def spread_y(half):
        for j in range(NZ):
            if j == 0:
                own_copies[half].wait()
            for source in ([2 * z + (1 - c)] if j == 0 else [2 * ring_z(j), 2 * ring_z(j) + 1]):
                z_copy(half, rem(zc - source, RING), source, source).wait_recv()
            y_copy(half, 0, j, y, up_y).start()
            y_copy(half, 1, j, y, down_y).start()

    def pass_y(half, first, last):
        for j in range(first, last):
            y_copy(half, 0, j, down_y, up_y).wait_recv()
            y_copy(half, 1, j, up_y, down_y).wait_recv()
            far_copy(half, j, up_y if j % 2 else down_y).start()

    lane = lax.broadcasted_iota(jnp.int32, (128, 128), 1).astype(F32)

    def gather(half, q):
        for p in range(QUAD):
            words = tok0[QUAD * q + p, PART:PART + TAB, :].astype(F32)
            each = TAB // NY
            mine = words[0:each]
            for group in range(1, NY):
                mine = jnp.where(y == group, words[group * each:(group + 1) * each], mine)
            for part_id in range(RING * QUAD * CAP // 128):
                column = jnp.broadcast_to(mine[part_id:part_id + 1, :], (128, 128)).T
                onehot[part_id * 128:(part_id + 1) * 128, p * 128:(p + 1) * 128] = jnp.where(
                    column == lane, 1.0, 0.0
                ).astype(BF16)
        blocks = jnp.concatenate([tok[half][QUAD * q + p, 0:PART, :] for p in range(QUAD)], axis=1)
        picked = lax.dot_general(
            onehot[...], blocks, (((1,), (1,)), ((), ())), preferred_element_type=F32
        ).astype(BF16)
        height = QUAD * CAP
        for e in range(RING):
            rows[half, e, pl.ds(pl.multiple_of(q * height, height), height), :] = picked[
                e * height:(e + 1) * height
            ]

    quads = RING // QUAD

    def gather_some(half, first, last):
        def body(step, carry):
            group = rem(y + lax.div(step, quads) - 1, NY)
            gather(half, group * quads + lax.rem(step, quads))
            return carry

        lax.fori_loop(first, last, body, 0)

    def place(i):
        j = lax.div(i, 2)
        half = lax.div(j + 1, 2)
        zj = rem(jnp.where(lax.rem(j, 2) == 1, z + half, z - half + NZ), NZ)
        core = rem(c + lax.rem(i, 2), 2)
        return 2 * zj + core

    def unit(u):
        i = jnp.where(u < 4, lax.rem(u, 2), lax.div(u, 2))
        half = jnp.where(u < 4, lax.div(u, 2), lax.rem(u, 2))
        return i, half

    def load(i):
        return pltpu.make_async_copy(gbuf.at[place(i)], gv.at[lax.rem(i, 2)], gl.at[lax.rem(i, 2)])

    def bring(i):
        j = lax.div(i, 2)
        index = place(i)
        other = lax.rem(i, 2) == 1
        for h in range(2):
            @pl.when(jnp.logical_and(other, j < NZ - 1))
            def _():
                ref = cut(gbuf.at[index], h)
                rdma(ref, ref, ss.at[j, h], sr.at[j, h], x, sibling).wait_recv()

            @pl.when(jnp.logical_and(other, j == NZ - 1))
            def _():
                pair_copy(8 - h, h, gbuf.at[index], index).wait_recv()

        load(i).start()

    mid = PART // 2
    top, bottom = pl.ds(0, mid), pl.ds(mid, mid)
    opposite = rem(x + 2, NX)

    def first_copies(u):
        slot = lax.rem(u, DEPTH)
        return (
            rdma(part.at[slot, opposite, top], r1.at[u, 0], s1s.at[u, 0], s1r.at[u, 0], up_x, me),
            rdma(part.at[slot, opposite, bottom], r1.at[u, 1], s1s.at[u, 1], s1r.at[u, 1], down_x, me),
        )

    def second_copies(u):
        slot = lax.rem(u, DEPTH)
        return (
            rdma(part.at[slot, up_x], r2.at[u, 0], s2s.at[u, 0], s2r.at[u, 0], up_x, me),
            rdma(part.at[slot, down_x], r2.at[u, 1], s2s.at[u, 1], s2r.at[u, 1], down_x, me),
        )

    def sent(u):
        for copy in first_copies(u):
            copy.wait_send()
        for copy in second_copies(u):
            copy.wait_send()

    def out_copies(u, remote, local):
        i, half = unit(u)
        slot = lax.rem(u, KEEP)
        for k in range(NY // HALVES):
            target = half * (NY // HALVES) + k
            away = rem(target - y, NY)

            @pl.when(away != 0)
            def _():
                remote(rdma(
                    total.at[slot, k], out.at[y * RING + place(i)],
                    cs.at[slot, k], cr.at[i, away], x, target * RING + zc,
                ))

            @pl.when(away == 0)
            def _():
                local(pltpu.make_async_copy(total.at[slot, k], out.at[y * RING + place(i)], cl.at[slot]))

    def give(u):
        out_copies(u, lambda copy: copy.start(), lambda copy: copy.start())

    def given(u):
        out_copies(u, lambda copy: copy.wait_send(), lambda copy: copy.wait())

    def multiply(u):
        i, half = unit(u)
        slot, held = lax.rem(u, DEPTH), lax.rem(i, 2)
        expert = place(i)

        @pl.when(u >= DEPTH)
        def _():
            sent(u - DEPTH)

        @pl.when(jnp.logical_or(u < 2, jnp.logical_and(u >= 4, lax.rem(u, 2) == 0)))
        def _():
            pltpu.make_async_copy(grad.at[0], gv.at[held], gl.at[held]).wait()

        for t in range(NX):
            part[slot, t] = lax.dot_general(
                rows[half, expert], gv[held, :, t * HSH:(t + 1) * HSH],
                (((0,), (0,)), ((), ())), preferred_element_type=F32,
            ).astype(BF16)
        for copy in first_copies(u):
            copy.start()

    def combine(u):
        slot = lax.rem(u, DEPTH)
        for copy in first_copies(u):
            copy.wait_recv()
        part[slot, up_x, top] = (
            part[slot, up_x, top].astype(F32) + r1[u, 0].astype(F32)
        ).astype(BF16)
        part[slot, down_x, bottom] = (
            part[slot, down_x, bottom].astype(F32) + r1[u, 1].astype(F32)
        ).astype(BF16)
        for copy in second_copies(u):
            copy.start()

    def finish(u):
        slot = lax.rem(u, DEPTH)

        @pl.when(u >= KEEP)
        def _():
            given(u - KEEP)

        for copy in second_copies(u):
            copy.wait_recv()
        for k in range(NY // HALVES):
            span = pl.ds(k * COLS, COLS)
            total[lax.rem(u, KEEP), k] = (
                part[slot, x, span].astype(F32)
                + r2[u, 0, span].astype(F32)
                + r2[u, 1, span].astype(F32)
            ).astype(BF16)
        give(u)

    def repeat(function):
        def body(u, carry):
            function(u)
            return carry

        lax.fori_loop(0, 2, body, 0)

    spread_y(0)
    pass_y(0, 0, NZ)
    spread_y(1)
    gather_some(0, 0, 3 * quads)
    for j in range(NZ):
        far_copy(0, j, far_y).wait_recv()
    gather_some(0, 3 * quads, 4 * quads)
    bring(jnp.int32(1))
    repeat(multiply)
    pass_y(1, 0, NZ // 2)
    repeat(combine)
    pass_y(1, NZ // 2, NZ)
    repeat(finish)
    gather_some(1, 0, 3 * quads)
    ring_step(1, 0)
    for j in range(NZ):
        far_copy(1, j, far_y).wait_recv()
    gather_some(1, 3 * quads, 4 * quads)

    def main_step(u, carry):
        following = lax.div(u, 2) + 1
        due = jnp.logical_and(lax.rem(u, 2) == 1, following < RING)
        fresh = lax.rem(following, 4) == 2

        @pl.when(jnp.logical_and(due, jnp.logical_not(fresh)))
        def _():
            bring(following)

        @pl.when(u < UNITS)
        def _():
            multiply(u)

        @pl.when(jnp.logical_and(u >= 4, u < UNITS + 2))
        def _():
            combine(u - 2)

        @pl.when(u >= 6)
        def _():
            finish(u - 4)

        for at, distance, h in ((3, 1, 1), (9, 2, 0), (11, 2, 1), (17, 3, 0), (19, 3, 1), (26, 4, 0), (27, 4, 1)):
            @pl.when(u == at)
            def _():
                ring_step(distance, h)

        @pl.when(jnp.logical_and(due, fresh))
        def _():
            bring(following)

        return carry

    lax.fori_loop(2, UNITS + 4, main_step, 0)

    def close(i, carry):
        for k in range(1, NY):
            source = rem(y - k, NY)
            rdma(
                total.at[0, 0], out.at[source * RING + place(i)],
                cs.at[0, 0], cr.at[i, k], x, source * RING + zc,
            ).wait_recv()
        return carry

    lax.fori_loop(0, RING, close, 0)

    def close_units(u, carry):
        sent(u)
        return carry

    def close_outs(u, carry):
        given(u)
        return carry

    lax.fori_loop(UNITS - DEPTH, UNITS, close_units, 0)
    lax.fori_loop(UNITS - KEEP, UNITS, close_outs, 0)
    for half in range(HALVES):
        for k in range(1, RING):
            z_copy(half, k, rem(zc + k, RING), zc).wait_send()
        for j in range(NZ):
            y_copy(half, 0, j, y, up_y).wait_send()
            y_copy(half, 1, j, y, down_y).wait_send()
            far_copy(half, j, up_y if j % 2 else down_y).wait_send()
    for j in range(0, 9):
        for h in range(2):
            if holds(j, h):
                if j > 0:
                    ring_copy(j, h, grad.at[0], own).wait_send()
                pair_copy(j, h, grad.at[0], own).wait_send()


def local(stash_codes, stash_scales, expert_ids, grad_rows):
    table = slot_table(expert_ids)
    vmem = pl.BlockSpec(memory_space=pltpu.VMEM)
    hbm = pl.BlockSpec(memory_space=pl.ANY)
    dma = pltpu.SemaphoreType.DMA
    weight_grad, _ = pl.pallas_call(
        kernel,
        out_shape=(
            jax.ShapeDtypeStruct((OWNERS, COLS, HSH), BF16),
            jax.ShapeDtypeStruct((RING, SLOTS, HW), BF16),
        ),
        in_specs=[hbm, vmem, vmem, hbm],
        out_specs=(hbm, hbm),
        scratch_shapes=[
            pltpu.VMEM((TOK, D), BF16),
            pltpu.VMEM((RING, PART + TAB, TOK), BF16),
            pltpu.VMEM((RING, PART, TOK), BF16),
            pltpu.VMEM((OWNERS, PART + TAB, TOK), BF16),
            pltpu.VMEM((OWNERS, PART, TOK), BF16),
            pltpu.VMEM((RING * QUAD * CAP, QUAD * TOK), BF16),
            pltpu.VMEM((HALVES, RING, SLOTS, PART), BF16),
            pltpu.VMEM((2, SLOTS, HW), BF16),
            pltpu.VMEM((DEPTH, NX, PART, HSH), BF16),
            pltpu.VMEM((UNITS, 2, PART // 2, HSH), BF16),
            pltpu.VMEM((UNITS, 2, PART, HSH), BF16),
            pltpu.VMEM((KEEP, NY // HALVES, COLS, HSH), BF16),
            dma((CUTS,)), dma((HALVES,)),
            dma((HALVES, RING)), dma((HALVES, RING)),
            dma((HALVES, 2, NZ)), dma((HALVES, 2, NZ)), dma((HALVES, NZ)), dma((HALVES, NZ)),
            dma((9, 2)), dma((9, 2)), dma((9, 2)), dma((9, 2)), dma((2,)),
            dma((UNITS, 2)), dma((UNITS, 2)), dma((UNITS, 2)), dma((UNITS, 2)),
            dma((KEEP, 2)), dma((RING, NY)), dma((KEEP,)),
        ],
        compiler_params=pltpu.CompilerParams(
            collective_id=0, has_side_effects=True, vmem_limit_bytes=58 * 1024 * 1024
        ),
        cost_estimate=pl.CostEstimate(
            flops=2 * SLOTS * D * HW, bytes_accessed=100_000_000, transcendentals=0
        ),
    )(stash_codes, stash_scales.T, table, grad_rows)
    return weight_grad


def solution(mesh):
    return jax.shard_map(
        local,
        mesh=mesh,
        in_specs=(
            P(("dp", "expert"), None),
            P(("dp", "expert"), None),
            P(("dp", "expert"), None),
            P(("dp", "expert"), None, None),
        ),
        out_specs=P(None, "expert", "dp"),
        check_vma=False,
    )
```

```python
import jax
import jax.numpy as jnp
from jax import lax
from jax.experimental import pallas as pl
from jax.experimental.pallas import tpu as pltpu
from jax.sharding import PartitionSpec as P

QB = 128
EXP_DEV = 4
CAP = 12
D = 7168
HW = 1024
TOK = 128
NX, NY, NZ = 4, 4, 8
RING = 2 * NZ
OWNERS = NY * RING
COLS = D // OWNERS
WIDTH = NY * COLS
SLOTS = OWNERS * CAP
HSH = HW // NX
TOPK = 8
TAB = 16
HALVES = 2
PART = WIDTH // HALVES
UNITS = RING * HALVES
FIRST = 4
DEPTH = 6
KEEP = 4
CUTS = 4
QUAD = 4
MESH = pl.DeviceIdType.MESH
BF16 = jnp.bfloat16
F32 = jnp.float32


def rem(value, count):
    return lax.rem(value + count, count)


def kernel(
    codes, scales, ids, grad, out, gbuf,
    code, send0, send1, tok0, tok1, ranks, onehot, rows, gv, part, r1, r2, total,
    il, ol, zs, zr, ys, yr, yfs, yfr, gs, gr, ss, sr, gl,
    s1s, s1r, s2s, s2r, cs, cr, cl,
):
    x = lax.axis_index("dp")
    me = lax.axis_index("expert")
    y = lax.div(me, RING)
    zc = lax.rem(me, RING)
    z = lax.div(zc, 2)
    c = lax.rem(zc, 2)
    own = zc
    up_x, down_x = rem(x + 1, NX), rem(x - 1, NX)
    up_y, down_y = rem(y + 1, NY), rem(y - 1, NY)
    far_y = rem(y + 2, NY)
    dev_up_z = y * RING + 2 * rem(z + 1, NZ) + c
    dev_down_z = y * RING + 2 * rem(z - 1, NZ) + c
    sibling = y * RING + 2 * z + (1 - c)
    send, tok = (send0, send1), (tok0, tok1)

    def rdma(src, dst, send_sem, recv_sem, dev_x, dev_e):
        return pltpu.make_async_remote_copy(
            src_ref=src, dst_ref=dst, send_sem=send_sem, recv_sem=recv_sem,
            device_id=(dev_x, dev_e), device_id_type=MESH,
        )

    step = D // CUTS
    fetches = [
        pltpu.make_async_copy(
            codes.at[:, pl.ds(k * step, step)], code.at[:, pl.ds(k * step, step)], il.at[k]
        )
        for k in range(CUTS)
    ]
    for fetch in fetches:
        fetch.start()

    barrier = pltpu.get_barrier_semaphore()
    for k in range(1, RING):
        pl.semaphore_signal(barrier, inc=1, device_id=(x, y * RING + rem(zc + k, RING)), device_id_type=MESH)
    for k in range(1, NY):
        pl.semaphore_signal(barrier, inc=1, device_id=(x, rem(y + k, NY) * RING + zc), device_id_type=MESH)
    for dev_x in (up_x, down_x):
        pl.semaphore_signal(barrier, inc=1, device_id=(dev_x, me), device_id_type=MESH)

    row_id = lax.broadcasted_iota(jnp.int32, (QB, QB), 0)
    col_id = lax.broadcasted_iota(jnp.int32, (QB, QB), 1)
    common = row_id & col_id
    parity = jnp.zeros((QB, QB), jnp.int32)
    for bit in range(7):
        parity = parity + ((common >> bit) & 1)
    had = (1 - 2 * (parity & 1)).astype(F32).astype(BF16)

    def restore(half):
        blocks = D // QB // HALVES
        for k in range(half * blocks, (half + 1) * blocks):
            if k % (D // QB // CUTS) == 0:
                fetches[k // (D // QB // CUTS)].wait()
            turned = lax.dot_general(
                had, code[:, k * QB:(k + 1) * QB], (((1,), (1,)), ((), ())), preferred_element_type=F32
            )
            turned = (turned * (scales[k:k + 1, :] * QB ** (-0.5))).astype(BF16)
            start = 0
            while start < QB:
                n = k * QB + start
                idx, off = n // COLS, n % COLS
                length = min(QB - start, COLS - off)
                ty, tz = idx // RING, idx % RING
                at = (ty - half * (NY // HALVES)) * COLS + off
                send[half][tz, at:at + length, :] = turned[start:start + length]
                start += length

    def z_copy(half, k, target, source):
        return rdma(
            send[half].at[target], tok[half].at[y * RING + source],
            zs.at[half, k], zr.at[half, k], x, y * RING + target,
        )

    own_copies = [
        pltpu.make_async_copy(send[half].at[own], tok[half].at[me], ol.at[half]) for half in range(HALVES)
    ]

    def z_group(half, distance):
        for chip in ([z] if distance == 0 else [z + distance, z - distance][:1 if distance == NZ // 2 else 2]):
            for core in ([1 - c] if distance == 0 else [0, 1]):
                target = 2 * rem(chip, NZ) + core
                z_copy(half, rem(target - zc, RING), target, zc).start()

    named = jnp.concatenate(
        [ids[...].astype(F32), jnp.zeros((TAB - TOPK, TOK), F32)], axis=0
    ).astype(BF16)
    for k in range(RING):
        send0[k, PART:PART + TAB, :] = named
    def own_rows(h):
        span = pl.ds(h * (SLOTS // 2), SLOTS // 2)
        return rdma(grad.at[0, span], gbuf.at[own, span], ss.at[0, h], sr.at[0, h], x, sibling)

    for half in range(HALVES):
        restore(half)
        if half == 0:
            pl.semaphore_wait(barrier, RING - 1 + NY - 1 + 2)
        for distance in range(NZ // 2 + 1):
            z_group(half, distance)
        own_copies[half].start()
        if half == 0:
            for h in range(2):
                own_rows(h).start()

    def ring_z(j):
        return rem(z + (j + 1) // 2, NZ) if j % 2 else rem(z - j // 2, NZ)

    def cut(index, core, j):
        size = SLOTS // 2
        if j < 7:
            return gbuf.at[index, pl.ds(core * size, size)]
        return gbuf.at[index, pl.ds(core * size + (j % 2) * (size // 2), size // 2)]

    def ring_copy(j, k, source):
        ref = cut(2 * source + k, c, j)
        return rdma(ref, ref, gs.at[j, k], gr.at[j, k], x, dev_down_z if j % 2 else dev_up_z)

    def pair_copy(j, k, core):
        ref = cut(2 * ring_z(j) + k, core, j)
        return rdma(ref, ref, ss.at[j, k], sr.at[j, k], x, sibling)

    def others_rows(h):
        span = pl.ds(h * (SLOTS // 2), SLOTS // 2)
        index = 2 * z + (1 - c)
        return rdma(gbuf.at[index, span], gbuf.at[index, span], ss.at[0, h], sr.at[0, h], x, sibling)

    def own_copy(j):
        span = pl.ds(c * (SLOTS // 2), SLOTS // 2)
        return rdma(
            grad.at[0, span], gbuf.at[own, span], gs.at[j, c], gr.at[j, c],
            x, dev_down_z if j % 2 else dev_up_z,
        )

    def issue(n):
        distance, k = n // 2, n % 2
        for j in (2 * distance - 1, 2 * distance):
            if n >= 2:
                ring_copy(j + 2, k, ring_z(j)).start()
                continue

            @pl.when(c == k)
            def _():
                own_copy(j + 2).start()

            @pl.when(c != k)
            def _():
                ring_copy(j + 2, k, z).start()

    def arrive(n):
        distance, k = n // 2 + 1, n % 2
        for j in (2 * distance - 1, 2 * distance):
            ring_copy(j, k, ring_z(j)).wait_recv()
            pair_copy(j, k, c).start()

    def chunk(half, group, j):
        return tok[half].at[pl.ds(group * RING + 2 * ring_z(j), 2)]

    def y_copy(half, way, j, group, target):
        ref = chunk(half, group, j)
        return rdma(ref, ref, ys.at[half, way, j], yr.at[half, way, j], x, target * RING + zc)

    def far_copy(half, j, group):
        ref = chunk(half, group, j)
        target = down_y if j % 2 else up_y
        return rdma(ref, ref, yfs.at[half, j], yfr.at[half, j], x, target * RING + zc)

    def spread_y(half, first, last):
        for j in range(first, last):
            if j == 0:
                own_copies[half].wait()
            for source in ([2 * z + (1 - c)] if j == 0 else [2 * ring_z(j), 2 * ring_z(j) + 1]):
                z_copy(half, rem(zc - source, RING), source, source).wait_recv()
            y_copy(half, 0, j, y, up_y).start()
            y_copy(half, 1, j, y, down_y).start()

    def pass_y(half, first, last):
        for j in range(first, last):
            y_copy(half, 0, j, down_y, up_y).wait_recv()
            y_copy(half, 1, j, up_y, down_y).wait_recv()
            far_copy(half, j, up_y if j % 2 else down_y).start()

    before = jnp.where(
        lax.broadcasted_iota(jnp.int32, (TOK, TOK), 0) < lax.broadcasted_iota(jnp.int32, (TOK, TOK), 1),
        1.0, 0.0,
    ).astype(BF16)
    expert_id = (lax.broadcasted_iota(jnp.int32, (RING, TOK), 0) * EXP_DEV + y * (RING * EXP_DEV)).astype(F32)
    slot_row = lax.broadcasted_iota(jnp.int32, (QUAD * CAP, TOK), 0).astype(F32)

    def rank(q):
        members = []
        for p in range(QUAD):
            words = tok0[QUAD * q + p, PART:PART + TAB, :].astype(F32)
            member = jnp.zeros((RING, TOK), F32)
            for k in range(TOPK):
                member = jnp.where(expert_id == words[k:k + 1, :], 1.0, member)
            members.append(member)
        member = jnp.concatenate(members, axis=0)
        order = lax.dot_general(
            member.astype(BF16), before, (((1,), (0,)), ((), ())), preferred_element_type=F32
        )
        ranks[q] = jnp.where(member > 0.5, order, -100.0)

    def gather(half, q):
        if half == 0:
            rank(q)
        height = QUAD * CAP
        for p in range(QUAD):
            for e in range(RING):
                taken = ranks[q, p * RING + e:p * RING + e + 1, :]
                onehot[e * height:(e + 1) * height, p * TOK:(p + 1) * TOK] = jnp.where(
                    taken == slot_row - p * CAP, 1.0, 0.0
                ).astype(BF16)
        blocks = jnp.concatenate([tok[half][QUAD * q + p, 0:PART, :] for p in range(QUAD)], axis=1)
        picked = lax.dot_general(
            onehot[...], blocks, (((1,), (1,)), ((), ())), preferred_element_type=F32
        ).astype(BF16)
        for e in range(RING):
            rows[half, e, pl.ds(pl.multiple_of(q * height, height), height), :] = picked[
                e * height:(e + 1) * height
            ]

    quads = RING // QUAD

    def gather_some(half, first, last):
        def body(step, carry):
            turn = lax.div(step, quads)
            group = rem(y + jnp.where(turn == 3, 2, jnp.where(turn == 2, -1, turn)), NY)
            gather(half, group * quads + lax.rem(step, quads))
            return carry

        lax.fori_loop(first, last, body, 0)

    def way(i):
        past = jnp.maximum(i - 2, 0)
        distance = jnp.where(i < 2, 0, lax.div(past, 4) + 1)
        side = lax.rem(past, 2)
        core = jnp.where(jnp.logical_or(i < 2, i == RING - 1), lax.rem(i, 2), lax.div(lax.rem(past, 4), 2))
        return distance, side, core

    def place(i):
        distance, side, core = way(i)
        return 2 * rem(jnp.where(side == 0, z + distance, z - distance + NZ), NZ) + core

    def unit(u):
        early = u < 2 * FIRST
        i = jnp.where(early, lax.rem(u, FIRST), lax.div(u, 2))
        half = jnp.where(early, lax.div(u, FIRST), lax.rem(u, 2))
        return i, half

    def load(i):
        slot = lax.rem(i, FIRST)
        return pltpu.make_async_copy(gbuf.at[place(i)], gv.at[slot], gl.at[slot])

    def bring(i):
        distance, side, core = way(i)
        index = place(i)
        size = SLOTS // 2

        @pl.when(distance < NZ // 2)
        def _():
            j = 2 * distance - 1 + side
            ref = gbuf.at[index, pl.ds((1 - c) * size, size)]
            rdma(ref, ref, ss.at[j, core], sr.at[j, core], x, sibling).wait_recv()

        @pl.when(distance == NZ // 2)
        def _():
            for j in (7, 8):
                ref = gbuf.at[index, pl.ds((1 - c) * size + (j % 2) * (size // 2), size // 2)]
                rdma(ref, ref, ss.at[j, core], sr.at[j, core], x, sibling).wait_recv()

        load(i).start()

    mid = PART // 2
    top, bottom = pl.ds(0, mid), pl.ds(mid, mid)
    opposite = rem(x + 2, NX)

    def first_copies(u):
        slot = lax.rem(u, DEPTH)
        return (
            rdma(part.at[slot, opposite, top], r1.at[u, 0], s1s.at[u, 0], s1r.at[u, 0], up_x, me),
            rdma(part.at[slot, opposite, bottom], r1.at[u, 1], s1s.at[u, 1], s1r.at[u, 1], down_x, me),
        )

    def second_copies(u):
        slot = lax.rem(u, DEPTH)
        return (
            rdma(part.at[slot, up_x], r2.at[u, 0], s2s.at[u, 0], s2r.at[u, 0], up_x, me),
            rdma(part.at[slot, down_x], r2.at[u, 1], s2s.at[u, 1], s2r.at[u, 1], down_x, me),
        )

    def sent(u):
        for copy in first_copies(u):
            copy.wait_send()
        for copy in second_copies(u):
            copy.wait_send()

    def out_copies(u, remote, local):
        i, half = unit(u)
        slot = lax.rem(u, KEEP)
        for k in range(NY // HALVES):
            target = half * (NY // HALVES) + k
            away = rem(target - y, NY)

            @pl.when(away != 0)
            def _():
                remote(rdma(
                    total.at[slot, k], out.at[y * RING + place(i)],
                    cs.at[slot, k], cr.at[i, away], x, target * RING + zc,
                ))

            @pl.when(away == 0)
            def _():
                local(pltpu.make_async_copy(total.at[slot, k], out.at[y * RING + place(i)], cl.at[slot]))

    def give(u):
        out_copies(u, lambda copy: copy.start(), lambda copy: copy.start())

    def given(u):
        out_copies(u, lambda copy: copy.wait_send(), lambda copy: copy.wait())

    def multiply(u):
        i, half = unit(u)
        slot, held = lax.rem(u, DEPTH), lax.rem(i, FIRST)
        expert = place(i)

        @pl.when(u >= DEPTH)
        def _():
            sent(u - DEPTH)

        @pl.when(jnp.logical_or(u < FIRST, jnp.logical_and(u >= 2 * FIRST, lax.rem(u, 2) == 0)))
        def _():
            pltpu.make_async_copy(grad.at[0], gv.at[held], gl.at[held]).wait()

        for t in range(NX):
            part[slot, t] = lax.dot_general(
                rows[half, expert], gv[held, :, t * HSH:(t + 1) * HSH],
                (((0,), (0,)), ((), ())), preferred_element_type=F32,
            ).astype(BF16)
        for copy in first_copies(u):
            copy.start()

    def combine(u):
        slot = lax.rem(u, DEPTH)
        for copy in first_copies(u):
            copy.wait_recv()
        part[slot, up_x, top] = (
            part[slot, up_x, top].astype(F32) + r1[u, 0].astype(F32)
        ).astype(BF16)
        part[slot, down_x, bottom] = (
            part[slot, down_x, bottom].astype(F32) + r1[u, 1].astype(F32)
        ).astype(BF16)
        for copy in second_copies(u):
            copy.start()

    def finish(u):
        slot = lax.rem(u, DEPTH)

        @pl.when(u >= KEEP)
        def _():
            given(u - KEEP)

        for copy in second_copies(u):
            copy.wait_recv()
        for k in range(NY // HALVES):
            span = pl.ds(k * COLS, COLS)
            total[lax.rem(u, KEEP), k] = (
                part[slot, x, span].astype(F32)
                + r2[u, 0, span].astype(F32)
                + r2[u, 1, span].astype(F32)
            ).astype(BF16)
        give(u)

    def repeat(function, first):
        def body(u, carry):
            function(u)
            return carry

        lax.fori_loop(first, first + 2, body, 0)

    def far_y_arrived(half):
        for j in range(NZ):
            far_copy(half, j, far_y).wait_recv()

    spread_y(0, 0, NZ)
    for h in range(2):
        others_rows(h).wait_recv()
    for core in range(2):
        @pl.when(c == core)
        def _():
            pltpu.make_async_copy(grad.at[0], gv.at[core], gl.at[core]).start()

        @pl.when(c != core)
        def _():
            load(jnp.int32(core)).start()

    issue(0)
    issue(1)
    gather_some(0, 0, quads)
    pass_y(0, 0, NZ)
    gather_some(0, quads, 3 * quads)
    spread_y(1, 0, NZ // 2)
    far_y_arrived(0)
    gather_some(0, 3 * quads, 4 * quads)
    repeat(multiply, 0)
    spread_y(1, NZ // 2, NZ)
    repeat(combine, 0)
    pass_y(1, 0, NZ // 2)
    repeat(finish, 0)
    gather_some(1, 0, quads)
    arrive(0)
    issue(2)
    bring(jnp.int32(2))
    bring(jnp.int32(3))
    repeat(multiply, 2)
    pass_y(1, NZ // 2, NZ)
    repeat(combine, 2)
    gather_some(1, quads, 3 * quads)
    far_y_arrived(1)
    gather_some(1, 3 * quads, 4 * quads)
    repeat(finish, 2)

    def main_step(u, carry):
        @pl.when(u < UNITS)
        def _():
            multiply(u)

        @pl.when(jnp.logical_and(u >= FIRST + 2, u < UNITS + 2))
        def _():
            combine(u - 2)

        @pl.when(u >= FIRST + 4)
        def _():
            finish(u - 4)

        for n, at in ((1, 6), (2, 10), (3, 14), (4, 18), (5, 22), (6, 26), (7, 28)):
            @pl.when(u == at)
            def _():
                arrive(n)
                if n + 2 < NZ:
                    issue(n + 2)

        following = lax.div(u, 2) + 1
        odd = jnp.logical_and(lax.rem(following, 2) == 1, following < RING - 1)
        due = jnp.where(odd, lax.rem(u, 2) == 0, lax.rem(u, 2) == 1)

        @pl.when(jnp.logical_and(due, jnp.logical_and(following >= FIRST, following < RING)))
        def _():
            bring(following)

        return carry

    lax.fori_loop(FIRST, UNITS + 4, main_step, 0)

    def close(i, carry):
        for k in range(1, NY):
            source = rem(y - k, NY)
            rdma(
                total.at[0, 0], out.at[source * RING + place(i)],
                cs.at[0, 0], cr.at[i, k], x, source * RING + zc,
            ).wait_recv()
        return carry

    lax.fori_loop(0, RING, close, 0)

    def close_units(u, carry):
        sent(u)
        return carry

    def close_outs(u, carry):
        given(u)
        return carry

    lax.fori_loop(UNITS - DEPTH, UNITS, close_units, 0)
    lax.fori_loop(UNITS - KEEP, UNITS, close_outs, 0)
    for half in range(HALVES):
        for k in range(1, RING):
            z_copy(half, k, rem(zc + k, RING), zc).wait_send()
        for j in range(NZ):
            y_copy(half, 0, j, y, up_y).wait_send()
            y_copy(half, 1, j, y, down_y).wait_send()
            far_copy(half, j, up_y if j % 2 else down_y).wait_send()
    for k in range(2):
        own_rows(k).wait_send()
        for j in range(1, 9):
            ring_copy(j, k, z).wait_send()
            pair_copy(j, k, c).wait_send()


def local(stash_codes, stash_scales, expert_ids, grad_rows):
    vmem = pl.BlockSpec(memory_space=pltpu.VMEM)
    hbm = pl.BlockSpec(memory_space=pl.ANY)
    dma = pltpu.SemaphoreType.DMA
    weight_grad, _ = pl.pallas_call(
        kernel,
        out_shape=(
            jax.ShapeDtypeStruct((OWNERS, COLS, HSH), BF16),
            jax.ShapeDtypeStruct((RING, SLOTS, HW), BF16),
        ),
        in_specs=[hbm, vmem, vmem, hbm],
        out_specs=(hbm, hbm),
        scratch_shapes=[
            pltpu.VMEM((TOK, D), BF16),
            pltpu.VMEM((RING, PART + TAB, TOK), BF16),
            pltpu.VMEM((RING, PART, TOK), BF16),
            pltpu.VMEM((OWNERS, PART + TAB, TOK), BF16),
            pltpu.VMEM((OWNERS, PART, TOK), BF16),
            pltpu.VMEM((OWNERS // QUAD, QUAD * RING, TOK), F32),
            pltpu.VMEM((RING * QUAD * CAP, QUAD * TOK), BF16),
            pltpu.VMEM((HALVES, RING, SLOTS, PART), BF16),
            pltpu.VMEM((FIRST, SLOTS, HW), BF16),
            pltpu.VMEM((DEPTH, NX, PART, HSH), BF16),
            pltpu.VMEM((UNITS, 2, PART // 2, HSH), BF16),
            pltpu.VMEM((UNITS, 2, PART, HSH), BF16),
            pltpu.VMEM((KEEP, NY // HALVES, COLS, HSH), BF16),
            dma((CUTS,)), dma((HALVES,)),
            dma((HALVES, RING)), dma((HALVES, RING)),
            dma((HALVES, 2, NZ)), dma((HALVES, 2, NZ)), dma((HALVES, NZ)), dma((HALVES, NZ)),
            dma((9, 2)), dma((9, 2)), dma((9, 2)), dma((9, 2)), dma((FIRST,)),
            dma((UNITS, 2)), dma((UNITS, 2)), dma((UNITS, 2)), dma((UNITS, 2)),
            dma((KEEP, 2)), dma((RING, NY)), dma((KEEP,)),
        ],
        compiler_params=pltpu.CompilerParams(
            collective_id=0, has_side_effects=True, vmem_limit_bytes=58 * 1024 * 1024
        ),
        cost_estimate=pl.CostEstimate(
            flops=2 * SLOTS * D * HW, bytes_accessed=100_000_000, transcendentals=0
        ),
    )(stash_codes, stash_scales.T, expert_ids.T, grad_rows)
    return weight_grad


def solution(mesh):
    return jax.shard_map(
        local,
        mesh=mesh,
        in_specs=(
            P(("dp", "expert"), None),
            P(("dp", "expert"), None),
            P(("dp", "expert"), None),
            P(("dp", "expert"), None, None),
        ),
        out_specs=P(None, "expert", "dp"),
        check_vma=False,
    )
```

```python
import jax
import jax.numpy as jnp
from jax import lax
from jax.experimental import pallas as pl
from jax.experimental.pallas import tpu as pltpu
from jax.sharding import PartitionSpec as P

QB = 128
EXP_DEV = 4
CAP = 12
D = 7168
HW = 1024
TOK = 128
NX, NY, NZ = 4, 4, 8
RING = 2 * NZ
OWNERS = NY * RING
COLS = D // OWNERS
WIDTH = NY * COLS
SLOTS = OWNERS * CAP
HSH = HW // NX
TOPK = 8
TAB = 16
HALVES = 2
PART = WIDTH // HALVES
UNITS = RING * HALVES
FIRST = 4
DEPTH = 6
KEEP = 4
CUTS = 4
QUAD = 4
MESH = pl.DeviceIdType.MESH
BF16 = jnp.bfloat16
F32 = jnp.float32


def rem(value, count):
    return lax.rem(value + count, count)


def kernel(
    codes, scales, ids, grad, out, gbuf,
    code, send0, send1, tok0, tok1, ranks, onehot, rows, gv, part, r1, r2, total,
    il, ol, zs, zr, ys, yr, yfs, yfr, gs, gr, ss, sr, gl,
    s1s, s1r, s2s, s2r, cs, cr, cl,
):
    x = lax.axis_index("dp")
    me = lax.axis_index("expert")
    y = lax.div(me, RING)
    zc = lax.rem(me, RING)
    z = lax.div(zc, 2)
    c = lax.rem(zc, 2)
    own = zc
    up_x, down_x = rem(x + 1, NX), rem(x - 1, NX)
    up_y, down_y = rem(y + 1, NY), rem(y - 1, NY)
    far_y = rem(y + 2, NY)
    dev_up_z = y * RING + 2 * rem(z + 1, NZ) + c
    dev_down_z = y * RING + 2 * rem(z - 1, NZ) + c
    sibling = y * RING + 2 * z + (1 - c)
    send, tok = (send0, send1), (tok0, tok1)

    def rdma(src, dst, send_sem, recv_sem, dev_x, dev_e):
        return pltpu.make_async_remote_copy(
            src_ref=src, dst_ref=dst, send_sem=send_sem, recv_sem=recv_sem,
            device_id=(dev_x, dev_e), device_id_type=MESH,
        )

    step = D // CUTS
    fetches = [
        pltpu.make_async_copy(
            codes.at[:, pl.ds(k * step, step)], code.at[:, pl.ds(k * step, step)], il.at[k]
        )
        for k in range(CUTS)
    ]
    for fetch in fetches:
        fetch.start()

    barrier = pltpu.get_barrier_semaphore()
    for k in range(1, RING):
        pl.semaphore_signal(barrier, inc=1, device_id=(x, y * RING + rem(zc + k, RING)), device_id_type=MESH)
    for k in range(1, NY):
        pl.semaphore_signal(barrier, inc=1, device_id=(x, rem(y + k, NY) * RING + zc), device_id_type=MESH)
    for dev_x in (up_x, down_x):
        pl.semaphore_signal(barrier, inc=1, device_id=(dev_x, me), device_id_type=MESH)

    row_id = lax.broadcasted_iota(jnp.int32, (QB, QB), 0)
    col_id = lax.broadcasted_iota(jnp.int32, (QB, QB), 1)
    common = row_id & col_id
    parity = jnp.zeros((QB, QB), jnp.int32)
    for bit in range(7):
        parity = parity + ((common >> bit) & 1)
    had = (1 - 2 * (parity & 1)).astype(F32).astype(BF16)

    def restore(half):
        blocks = D // QB // HALVES
        for k in range(half * blocks, (half + 1) * blocks):
            if k % (D // QB // CUTS) == 0:
                fetches[k // (D // QB // CUTS)].wait()
            turned = lax.dot_general(
                had, code[:, k * QB:(k + 1) * QB], (((1,), (1,)), ((), ())), preferred_element_type=F32
            )
            turned = (turned * (scales[k:k + 1, :] * QB ** (-0.5))).astype(BF16)
            start = 0
            while start < QB:
                n = k * QB + start
                idx, off = n // COLS, n % COLS
                length = min(QB - start, COLS - off)
                ty, tz = idx // RING, idx % RING
                at = (ty - half * (NY // HALVES)) * COLS + off
                send[half][tz, at:at + length, :] = turned[start:start + length]
                start += length

    def z_copy(half, k, target, source):
        return rdma(
            send[half].at[target], tok[half].at[y * RING + source],
            zs.at[half, k], zr.at[half, k], x, y * RING + target,
        )

    own_copies = [
        pltpu.make_async_copy(send[half].at[own], tok[half].at[me], ol.at[half]) for half in range(HALVES)
    ]

    def z_group(half, distance):
        for chip in ([z] if distance == 0 else [z + distance, z - distance][:1 if distance == NZ // 2 else 2]):
            for core in ([1 - c] if distance == 0 else [0, 1]):
                target = 2 * rem(chip, NZ) + core
                z_copy(half, rem(target - zc, RING), target, zc).start()

    named = jnp.concatenate(
        [ids[...].astype(F32), jnp.zeros((TAB - TOPK, TOK), F32)], axis=0
    ).astype(BF16)
    for k in range(RING):
        send0[k, PART:PART + TAB, :] = named
    def own_rows(h):
        span = pl.ds(h * (SLOTS // 2), SLOTS // 2)
        return rdma(grad.at[0, span], gbuf.at[own, span], ss.at[0, h], sr.at[0, h], x, sibling)

    for half in range(HALVES):
        restore(half)
        if half == 0:
            pl.semaphore_wait(barrier, RING - 1 + NY - 1 + 2)
        for distance in range(NZ // 2 + 1):
            z_group(half, distance)
        own_copies[half].start()
        if half == 0:
            for h in range(2):
                own_rows(h).start()

    def ring_z(j):
        return rem(z + (j + 1) // 2, NZ) if j % 2 else rem(z - j // 2, NZ)

    def cut(index, core, j):
        size = SLOTS // 2
        if j < 7:
            return gbuf.at[index, pl.ds(core * size, size)]
        return gbuf.at[index, pl.ds(core * size + (j % 2) * (size // 2), size // 2)]

    def ring_copy(j, k, source):
        ref = cut(2 * source + k, c, j)
        return rdma(ref, ref, gs.at[j, k], gr.at[j, k], x, dev_down_z if j % 2 else dev_up_z)

    def pair_copy(j, k, core):
        ref = cut(2 * ring_z(j) + k, core, j)
        return rdma(ref, ref, ss.at[j, k], sr.at[j, k], x, sibling)

    def others_rows(h):
        span = pl.ds(h * (SLOTS // 2), SLOTS // 2)
        index = 2 * z + (1 - c)
        return rdma(gbuf.at[index, span], gbuf.at[index, span], ss.at[0, h], sr.at[0, h], x, sibling)

    def own_copy(j):
        span = pl.ds(c * (SLOTS // 2), SLOTS // 2)
        return rdma(
            grad.at[0, span], gbuf.at[own, span], gs.at[j, c], gr.at[j, c],
            x, dev_down_z if j % 2 else dev_up_z,
        )

    def issue(n):
        distance, k = n // 2, n % 2
        for j in (2 * distance - 1, 2 * distance):
            if n >= 2:
                ring_copy(j + 2, k, ring_z(j)).start()
                continue

            @pl.when(c == k)
            def _():
                own_copy(j + 2).start()

            @pl.when(c != k)
            def _():
                ring_copy(j + 2, k, z).start()

    def arrive(n):
        distance, k = n // 2 + 1, n % 2
        for j in (2 * distance - 1, 2 * distance):
            ring_copy(j, k, ring_z(j)).wait_recv()
            pair_copy(j, k, c).start()

    def chunk(half, group, j):
        return tok[half].at[pl.ds(group * RING + 2 * ring_z(j), 2)]

    def y_copy(half, way, j, group, target):
        ref = chunk(half, group, j)
        return rdma(ref, ref, ys.at[half, way, j], yr.at[half, way, j], x, target * RING + zc)

    def far_copy(half, j, group):
        ref = chunk(half, group, j)
        target = down_y if j % 2 else up_y
        return rdma(ref, ref, yfs.at[half, j], yfr.at[half, j], x, target * RING + zc)

    def spread_y(half, first, last):
        for j in range(first, last):
            if j == 0:
                own_copies[half].wait()
            for source in ([2 * z + (1 - c)] if j == 0 else [2 * ring_z(j), 2 * ring_z(j) + 1]):
                z_copy(half, rem(zc - source, RING), source, source).wait_recv()
            y_copy(half, 0, j, y, up_y).start()
            y_copy(half, 1, j, y, down_y).start()

    def pass_y(half, first, last):
        for j in range(first, last):
            y_copy(half, 0, j, down_y, up_y).wait_recv()
            y_copy(half, 1, j, up_y, down_y).wait_recv()
            far_copy(half, j, up_y if j % 2 else down_y).start()

    before = jnp.where(
        lax.broadcasted_iota(jnp.int32, (TOK, TOK), 0) < lax.broadcasted_iota(jnp.int32, (TOK, TOK), 1),
        1.0, 0.0,
    ).astype(BF16)
    expert_id = (lax.broadcasted_iota(jnp.int32, (RING, TOK), 0) * EXP_DEV + y * (RING * EXP_DEV)).astype(F32)
    slot_row = lax.broadcasted_iota(jnp.int32, (QUAD * CAP, TOK), 0).astype(F32)

    def rank(q):
        members = []
        for p in range(QUAD):
            words = tok0[QUAD * q + p, PART:PART + TAB, :].astype(F32)
            member = jnp.zeros((RING, TOK), F32)
            for k in range(TOPK):
                member = jnp.where(expert_id == words[k:k + 1, :], 1.0, member)
            members.append(member)
        member = jnp.concatenate(members, axis=0)
        order = lax.dot_general(
            member.astype(BF16), before, (((1,), (0,)), ((), ())), preferred_element_type=F32
        )
        ranks[q] = jnp.where(member > 0.5, order, -100.0)

    def gather(half, q):
        if half == 0:
            rank(q)
        height = QUAD * CAP
        for p in range(QUAD):
            for e in range(RING):
                taken = ranks[q, p * RING + e:p * RING + e + 1, :]
                onehot[e * height:(e + 1) * height, p * TOK:(p + 1) * TOK] = jnp.where(
                    taken == slot_row - p * CAP, 1.0, 0.0
                ).astype(BF16)
        blocks = jnp.concatenate([tok[half][QUAD * q + p, 0:PART, :] for p in range(QUAD)], axis=1)
        picked = lax.dot_general(
            onehot[...], blocks, (((1,), (1,)), ((), ())), preferred_element_type=F32
        ).astype(BF16)
        for e in range(RING):
            rows[half, e, pl.ds(pl.multiple_of(q * height, height), height), :] = picked[
                e * height:(e + 1) * height
            ]

    quads = RING // QUAD

    def gather_some(half, first, last):
        def body(step, carry):
            turn = lax.div(step, quads)
            group = rem(y + jnp.where(turn == 3, 2, jnp.where(turn == 2, -1, turn)), NY)
            gather(half, group * quads + lax.rem(step, quads))
            return carry

        lax.fori_loop(first, last, body, 0)

    def way(i):
        past = jnp.maximum(i - 2, 0)
        distance = jnp.where(i < 2, 0, lax.div(past, 4) + 1)
        side = lax.rem(past, 2)
        core = jnp.where(jnp.logical_or(i < 2, i == RING - 1), lax.rem(i, 2), lax.div(lax.rem(past, 4), 2))
        return distance, side, core

    def place(i):
        distance, side, core = way(i)
        return 2 * rem(jnp.where(side == 0, z + distance, z - distance + NZ), NZ) + core

    def unit(u):
        early = u < 2 * FIRST
        i = jnp.where(early, lax.rem(u, FIRST), lax.div(u, 2))
        half = jnp.where(early, lax.div(u, FIRST), lax.rem(u, 2))
        return i, half

    def load(i):
        slot = lax.rem(i, FIRST)
        return pltpu.make_async_copy(gbuf.at[place(i)], gv.at[slot], gl.at[slot])

    def bring(i):
        distance, side, core = way(i)
        index = place(i)
        size = SLOTS // 2

        @pl.when(distance < NZ // 2)
        def _():
            j = 2 * distance - 1 + side
            ref = gbuf.at[index, pl.ds((1 - c) * size, size)]
            rdma(ref, ref, ss.at[j, core], sr.at[j, core], x, sibling).wait_recv()

        @pl.when(distance == NZ // 2)
        def _():
            for j in (7, 8):
                ref = gbuf.at[index, pl.ds((1 - c) * size + (j % 2) * (size // 2), size // 2)]
                rdma(ref, ref, ss.at[j, core], sr.at[j, core], x, sibling).wait_recv()

        load(i).start()

    mid = PART // 2
    top, bottom = pl.ds(0, mid), pl.ds(mid, mid)
    opposite = rem(x + 2, NX)

    def first_copies(u):
        slot = lax.rem(u, DEPTH)
        return (
            rdma(part.at[slot, opposite, top], r1.at[u, 0], s1s.at[u, 0], s1r.at[u, 0], up_x, me),
            rdma(part.at[slot, opposite, bottom], r1.at[u, 1], s1s.at[u, 1], s1r.at[u, 1], down_x, me),
        )

    def second_copies(u):
        slot = lax.rem(u, DEPTH)
        return (
            rdma(part.at[slot, up_x], r2.at[u, 0], s2s.at[u, 0], s2r.at[u, 0], up_x, me),
            rdma(part.at[slot, down_x], r2.at[u, 1], s2s.at[u, 1], s2r.at[u, 1], down_x, me),
        )

    def sent(u):
        for copy in first_copies(u):
            copy.wait_send()
        for copy in second_copies(u):
            copy.wait_send()

    def out_copies(u, remote, local):
        i, half = unit(u)
        slot = lax.rem(u, KEEP)
        for k in range(NY // HALVES):
            target = half * (NY // HALVES) + k
            away = rem(target - y, NY)

            @pl.when(away != 0)
            def _():
                remote(rdma(
                    total.at[slot, k], out.at[y * RING + place(i)],
                    cs.at[slot, k], cr.at[i, away], x, target * RING + zc,
                ))

            @pl.when(away == 0)
            def _():
                local(pltpu.make_async_copy(total.at[slot, k], out.at[y * RING + place(i)], cl.at[slot]))

    def give(u):
        out_copies(u, lambda copy: copy.start(), lambda copy: copy.start())

    def given(u):
        out_copies(u, lambda copy: copy.wait_send(), lambda copy: copy.wait())

    def multiply(u):
        i, half = unit(u)
        slot, held = lax.rem(u, DEPTH), lax.rem(i, FIRST)
        expert = place(i)

        @pl.when(u >= DEPTH)
        def _():
            sent(u - DEPTH)

        @pl.when(jnp.logical_or(u < FIRST, jnp.logical_and(u >= 2 * FIRST, lax.rem(u, 2) == 0)))
        def _():
            pltpu.make_async_copy(grad.at[0], gv.at[held], gl.at[held]).wait()

        for t in range(NX):
            part[slot, t] = lax.dot_general(
                rows[half, expert], gv[held, :, t * HSH:(t + 1) * HSH],
                (((0,), (0,)), ((), ())), preferred_element_type=F32,
            ).astype(BF16)
        for copy in first_copies(u):
            copy.start()

    def combine(u):
        slot = lax.rem(u, DEPTH)
        for copy in first_copies(u):
            copy.wait_recv()
        part[slot, up_x, top] = (
            part[slot, up_x, top].astype(F32) + r1[u, 0].astype(F32)
        ).astype(BF16)
        part[slot, down_x, bottom] = (
            part[slot, down_x, bottom].astype(F32) + r1[u, 1].astype(F32)
        ).astype(BF16)
        for copy in second_copies(u):
            copy.start()

    def finish(u):
        slot = lax.rem(u, DEPTH)

        @pl.when(u >= KEEP)
        def _():
            given(u - KEEP)

        for copy in second_copies(u):
            copy.wait_recv()
        for k in range(NY // HALVES):
            span = pl.ds(k * COLS, COLS)
            total[lax.rem(u, KEEP), k] = (
                part[slot, x, span].astype(F32)
                + r2[u, 0, span].astype(F32)
                + r2[u, 1, span].astype(F32)
            ).astype(BF16)
        give(u)

    def repeat(function, first):
        def body(u, carry):
            function(u)
            return carry

        lax.fori_loop(first, first + 2, body, 0)

    def far_y_arrived(half):
        for j in range(NZ):
            far_copy(half, j, far_y).wait_recv()

    spread_y(0, 0, NZ)
    for h in range(2):
        others_rows(h).wait_recv()
    for core in range(2):
        @pl.when(c == core)
        def _():
            pltpu.make_async_copy(grad.at[0], gv.at[core], gl.at[core]).start()

        @pl.when(c != core)
        def _():
            load(jnp.int32(core)).start()

    issue(0)
    issue(1)
    gather_some(0, 0, quads)
    pass_y(0, 0, NZ)
    gather_some(0, quads, 3 * quads)
    spread_y(1, 0, NZ // 2)
    far_y_arrived(0)
    gather_some(0, 3 * quads, 4 * quads)
    repeat(multiply, 0)
    spread_y(1, NZ // 2, NZ)
    repeat(combine, 0)
    pass_y(1, 0, NZ // 2)
    repeat(finish, 0)
    gather_some(1, 0, quads)
    arrive(0)
    issue(2)
    bring(jnp.int32(2))
    bring(jnp.int32(3))
    repeat(multiply, 2)
    pass_y(1, NZ // 2, NZ)
    repeat(combine, 2)
    gather_some(1, quads, 3 * quads)
    far_y_arrived(1)
    gather_some(1, 3 * quads, 4 * quads)
    repeat(finish, 2)

    def main_step(u, carry):
        @pl.when(u < UNITS)
        def _():
            multiply(u)

        @pl.when(jnp.logical_and(u >= FIRST + 2, u < UNITS + 2))
        def _():
            combine(u - 2)

        @pl.when(u >= FIRST + 4)
        def _():
            finish(u - 4)

        for n, at in ((1, 6), (2, 10), (3, 14), (4, 18), (5, 22), (6, 26), (7, 28)):
            @pl.when(u == at)
            def _():
                arrive(n)
                if n + 2 < NZ:
                    issue(n + 2)

        following = lax.div(u, 2) + 1
        odd = jnp.logical_and(lax.rem(following, 2) == 1, following < RING - 1)
        due = jnp.where(odd, lax.rem(u, 2) == 0, lax.rem(u, 2) == 1)

        @pl.when(jnp.logical_and(due, jnp.logical_and(following >= FIRST, following < RING)))
        def _():
            bring(following)

        return carry

    lax.fori_loop(FIRST, UNITS + 4, main_step, 0)

    def close(i, carry):
        for k in range(1, NY):
            source = rem(y - k, NY)
            rdma(
                total.at[0, 0], out.at[source * RING + place(i)],
                cs.at[0, 0], cr.at[i, k], x, source * RING + zc,
            ).wait_recv()
        return carry

    lax.fori_loop(0, RING, close, 0)

    def close_units(u, carry):
        sent(u)
        return carry

    def close_outs(u, carry):
        given(u)
        return carry

    lax.fori_loop(UNITS - DEPTH, UNITS, close_units, 0)
    lax.fori_loop(UNITS - KEEP, UNITS, close_outs, 0)
    for half in range(HALVES):
        for k in range(1, RING):
            z_copy(half, k, rem(zc + k, RING), zc).wait_send()
        for j in range(NZ):
            y_copy(half, 0, j, y, up_y).wait_send()
            y_copy(half, 1, j, y, down_y).wait_send()
            far_copy(half, j, up_y if j % 2 else down_y).wait_send()
    for k in range(2):
        own_rows(k).wait_send()
        for j in range(1, 9):
            ring_copy(j, k, z).wait_send()
            pair_copy(j, k, c).wait_send()


def local(stash_codes, stash_scales, expert_ids, grad_rows):
    vmem = pl.BlockSpec(memory_space=pltpu.VMEM)
    hbm = pl.BlockSpec(memory_space=pl.ANY)
    dma = pltpu.SemaphoreType.DMA
    weight_grad, _ = pl.pallas_call(
        kernel,
        out_shape=(
            pltpu.VMEM((OWNERS, COLS, HSH), BF16),
            jax.ShapeDtypeStruct((RING, SLOTS, HW), BF16),
        ),
        in_specs=[hbm, vmem, vmem, hbm],
        out_specs=(vmem, hbm),
        scratch_shapes=[
            pltpu.VMEM((TOK, D), BF16),
            pltpu.VMEM((RING, PART + TAB, TOK), BF16),
            pltpu.VMEM((RING, PART, TOK), BF16),
            pltpu.VMEM((OWNERS, PART + TAB, TOK), BF16),
            pltpu.VMEM((OWNERS, PART, TOK), BF16),
            pltpu.VMEM((OWNERS // QUAD, QUAD * RING, TOK), F32),
            pltpu.VMEM((RING * QUAD * CAP, QUAD * TOK), BF16),
            pltpu.VMEM((HALVES, RING, SLOTS, PART), BF16),
            pltpu.VMEM((FIRST, SLOTS, HW), BF16),
            pltpu.VMEM((DEPTH, NX, PART, HSH), BF16),
            pltpu.VMEM((UNITS, 2, PART // 2, HSH), BF16),
            pltpu.VMEM((UNITS, 2, PART, HSH), BF16),
            pltpu.VMEM((KEEP, NY // HALVES, COLS, HSH), BF16),
            dma((CUTS,)), dma((HALVES,)),
            dma((HALVES, RING)), dma((HALVES, RING)),
            dma((HALVES, 2, NZ)), dma((HALVES, 2, NZ)), dma((HALVES, NZ)), dma((HALVES, NZ)),
            dma((9, 2)), dma((9, 2)), dma((9, 2)), dma((9, 2)), dma((FIRST,)),
            dma((UNITS, 2)), dma((UNITS, 2)), dma((UNITS, 2)), dma((UNITS, 2)),
            dma((KEEP, 2)), dma((RING, NY)), dma((KEEP,)),
        ],
        compiler_params=pltpu.CompilerParams(
            collective_id=0, has_side_effects=True, vmem_limit_bytes=56 * 1024 * 1024
        ),
        cost_estimate=pl.CostEstimate(
            flops=2 * SLOTS * D * HW, bytes_accessed=100_000_000, transcendentals=0
        ),
    )(stash_codes, stash_scales.T, expert_ids.T, grad_rows)
    return weight_grad


def solution(mesh):
    return jax.shard_map(
        local,
        mesh=mesh,
        in_specs=(
            P(("dp", "expert"), None),
            P(("dp", "expert"), None),
            P(("dp", "expert"), None),
            P(("dp", "expert"), None, None),
        ),
        out_specs=P(None, "expert", "dp"),
        check_vma=False,
    )
```

```python
import jax
import jax.numpy as jnp
from jax import lax
from jax.experimental import pallas as pl
from jax.experimental.pallas import tpu as pltpu
from jax.sharding import PartitionSpec as P

QB = 128
EXP_DEV = 4
CAP = 12
D = 7168
HW = 1024
TOK = 128
NX, NY, NZ = 4, 4, 8
RING = 2 * NZ
OWNERS = NY * RING
COLS = D // OWNERS
WIDTH = NY * COLS
SLOTS = OWNERS * CAP
HSH = HW // NX
TOPK = 8
TAB = 16
HALVES = 2
PART = WIDTH // HALVES
UNITS = RING * HALVES
FIRST = 4
DEPTH = 6
KEEP = 4
CUTS = 4
QUAD = 4
MESH = pl.DeviceIdType.MESH
BF16 = jnp.bfloat16
F32 = jnp.float32


def rem(value, count):
    return lax.rem(value + count, count)


def kernel(
    codes, scales, ids, grad, out, gbuf,
    code, send0, send1, tok0, tok1, ranks, onehot, rows, gv, part, r1, r2, total,
    il, ol, zs, zr, ys, yr, yfs, yfr, gs, gr, ss, sr, gl,
    s1s, s1r, s2s, s2r, cs, cr, cl,
):
    x = lax.axis_index("dp")
    me = lax.axis_index("expert")
    y = lax.div(me, RING)
    zc = lax.rem(me, RING)
    z = lax.div(zc, 2)
    c = lax.rem(zc, 2)
    own = zc
    up_x, down_x = rem(x + 1, NX), rem(x - 1, NX)
    up_y, down_y = rem(y + 1, NY), rem(y - 1, NY)
    far_y = rem(y + 2, NY)
    dev_up_z = y * RING + 2 * rem(z + 1, NZ) + c
    dev_down_z = y * RING + 2 * rem(z - 1, NZ) + c
    sibling = y * RING + 2 * z + (1 - c)
    send, tok = (send0, send1), (tok0, tok1)

    def rdma(src, dst, send_sem, recv_sem, dev_x, dev_e):
        return pltpu.make_async_remote_copy(
            src_ref=src, dst_ref=dst, send_sem=send_sem, recv_sem=recv_sem,
            device_id=(dev_x, dev_e), device_id_type=MESH,
        )

    step = D // CUTS
    fetches = [
        pltpu.make_async_copy(
            codes.at[:, pl.ds(k * step, step)], code.at[:, pl.ds(k * step, step)], il.at[k]
        )
        for k in range(CUTS)
    ]
    for fetch in fetches:
        fetch.start()

    barrier = pltpu.get_barrier_semaphore()
    for k in range(1, RING):
        pl.semaphore_signal(barrier, inc=1, device_id=(x, y * RING + rem(zc + k, RING)), device_id_type=MESH)
    for k in range(1, NY):
        pl.semaphore_signal(barrier, inc=1, device_id=(x, rem(y + k, NY) * RING + zc), device_id_type=MESH)
    for dev_x in (up_x, down_x):
        pl.semaphore_signal(barrier, inc=1, device_id=(dev_x, me), device_id_type=MESH)

    row_id = lax.broadcasted_iota(jnp.int32, (QB, QB), 0)
    col_id = lax.broadcasted_iota(jnp.int32, (QB, QB), 1)
    common = row_id & col_id
    parity = jnp.zeros((QB, QB), jnp.int32)
    for bit in range(7):
        parity = parity + ((common >> bit) & 1)
    had = (1 - 2 * (parity & 1)).astype(F32).astype(BF16)

    def restore(half):
        blocks = D // QB // HALVES
        for k in range(half * blocks, (half + 1) * blocks):
            if k % (D // QB // CUTS) == 0:
                fetches[k // (D // QB // CUTS)].wait()
            turned = lax.dot_general(
                had, code[:, k * QB:(k + 1) * QB], (((1,), (1,)), ((), ())), preferred_element_type=F32
            )
            turned = (turned * (scales[k:k + 1, :] * QB ** (-0.5))).astype(BF16)
            start = 0
            while start < QB:
                n = k * QB + start
                idx, off = n // COLS, n % COLS
                length = min(QB - start, COLS - off)
                ty, tz = idx // RING, idx % RING
                at = (ty - half * (NY // HALVES)) * COLS + off
                send[half][tz, at:at + length, :] = turned[start:start + length]
                start += length

    def z_copy(half, k, target, source):
        return rdma(
            send[half].at[target], tok[half].at[y * RING + source],
            zs.at[half, k], zr.at[half, k], x, y * RING + target,
        )

    own_copies = [
        pltpu.make_async_copy(send[half].at[own], tok[half].at[me], ol.at[half]) for half in range(HALVES)
    ]

    def z_group(half, distance):
        for chip in ([z] if distance == 0 else [z + distance, z - distance][:1 if distance == NZ // 2 else 2]):
            for core in ([1 - c] if distance == 0 else [0, 1]):
                target = 2 * rem(chip, NZ) + core
                z_copy(half, rem(target - zc, RING), target, zc).start()

    named = jnp.concatenate(
        [ids[...].astype(F32), jnp.zeros((TAB - TOPK, TOK), F32)], axis=0
    ).astype(BF16)
    for k in range(RING):
        send0[k, PART:PART + TAB, :] = named
    def own_rows(h):
        span = pl.ds(h * (SLOTS // 2), SLOTS // 2)
        return rdma(grad.at[0, span], gbuf.at[own, span], ss.at[0, h], sr.at[0, h], x, sibling)

    for half in range(HALVES):
        restore(half)
        if half == 0:
            pl.semaphore_wait(barrier, RING - 1 + NY - 1 + 2)
        for distance in range(NZ // 2 + 1):
            z_group(half, distance)
        own_copies[half].start()
        if half == 0:
            for h in range(2):
                own_rows(h).start()

    def ring_z(j):
        return rem(z + (j + 1) // 2, NZ) if j % 2 else rem(z - j // 2, NZ)

    def cut(index, core, j):
        size = SLOTS // 2
        if j < 7:
            return gbuf.at[index, pl.ds(core * size, size)]
        return gbuf.at[index, pl.ds(core * size + (j % 2) * (size // 2), size // 2)]

    def ring_copy(j, k, source):
        ref = cut(2 * source + k, c, j)
        return rdma(ref, ref, gs.at[j, k], gr.at[j, k], x, dev_down_z if j % 2 else dev_up_z)

    def pair_copy(j, k, core):
        ref = cut(2 * ring_z(j) + k, core, j)
        return rdma(ref, ref, ss.at[j, k], sr.at[j, k], x, sibling)

    def others_rows(h):
        span = pl.ds(h * (SLOTS // 2), SLOTS // 2)
        index = 2 * z + (1 - c)
        return rdma(gbuf.at[index, span], gbuf.at[index, span], ss.at[0, h], sr.at[0, h], x, sibling)

    def own_copy(j):
        span = pl.ds(c * (SLOTS // 2), SLOTS // 2)
        return rdma(
            grad.at[0, span], gbuf.at[own, span], gs.at[j, c], gr.at[j, c],
            x, dev_down_z if j % 2 else dev_up_z,
        )

    def issue(n):
        distance, k = n // 2, n % 2
        for j in (2 * distance - 1, 2 * distance):
            if n >= 2:
                ring_copy(j + 2, k, ring_z(j)).start()
                continue

            @pl.when(c == k)
            def _():
                own_copy(j + 2).start()

            @pl.when(c != k)
            def _():
                ring_copy(j + 2, k, z).start()

    def arrive(n):
        distance, k = n // 2 + 1, n % 2
        for j in (2 * distance - 1, 2 * distance):
            ring_copy(j, k, ring_z(j)).wait_recv()
            pair_copy(j, k, c).start()

    def chunk(half, group, j):
        return tok[half].at[pl.ds(group * RING + 2 * ring_z(j), 2)]

    def y_copy(half, way, j, group, target):
        ref = chunk(half, group, j)
        return rdma(ref, ref, ys.at[half, way, j], yr.at[half, way, j], x, target * RING + zc)

    def far_copy(half, j, group):
        ref = chunk(half, group, j)
        target = down_y if j % 2 else up_y
        return rdma(ref, ref, yfs.at[half, j], yfr.at[half, j], x, target * RING + zc)

    def spread_y(half, first, last):
        for j in range(first, last):
            if j == 0:
                own_copies[half].wait()
            for source in ([2 * z + (1 - c)] if j == 0 else [2 * ring_z(j), 2 * ring_z(j) + 1]):
                z_copy(half, rem(zc - source, RING), source, source).wait_recv()
            y_copy(half, 0, j, y, up_y).start()
            y_copy(half, 1, j, y, down_y).start()

    def pass_y(half, first, last):
        for j in range(first, last):
            y_copy(half, 0, j, down_y, up_y).wait_recv()
            y_copy(half, 1, j, up_y, down_y).wait_recv()
            far_copy(half, j, up_y if j % 2 else down_y).start()

    before = jnp.where(
        lax.broadcasted_iota(jnp.int32, (TOK, TOK), 0) < lax.broadcasted_iota(jnp.int32, (TOK, TOK), 1),
        1.0, 0.0,
    ).astype(BF16)
    expert_id = (lax.broadcasted_iota(jnp.int32, (RING, TOK), 0) * EXP_DEV + y * (RING * EXP_DEV)).astype(F32)
    slot_row = lax.broadcasted_iota(jnp.int32, (QUAD * CAP, TOK), 0).astype(F32)

    def rank(q):
        members = []
        for p in range(QUAD):
            words = tok0[QUAD * q + p, PART:PART + TAB, :].astype(F32)
            member = jnp.zeros((RING, TOK), F32)
            for k in range(TOPK):
                member = jnp.where(expert_id == words[k:k + 1, :], 1.0, member)
            members.append(member)
        member = jnp.concatenate(members, axis=0)
        order = lax.dot_general(
            member.astype(BF16), before, (((1,), (0,)), ((), ())), preferred_element_type=F32
        )
        ranks[q] = jnp.where(member > 0.5, order, -100.0)

    def gather(half, q):
        if half == 0:
            rank(q)
        height = QUAD * CAP
        for p in range(QUAD):
            for e in range(RING):
                taken = ranks[q, p * RING + e:p * RING + e + 1, :]
                onehot[e * height:(e + 1) * height, p * TOK:(p + 1) * TOK] = jnp.where(
                    taken == slot_row - p * CAP, 1.0, 0.0
                ).astype(BF16)
        blocks = jnp.concatenate([tok[half][QUAD * q + p, 0:PART, :] for p in range(QUAD)], axis=1)
        picked = lax.dot_general(
            onehot[...], blocks, (((1,), (1,)), ((), ())), preferred_element_type=F32
        ).astype(BF16)
        for e in range(RING):
            rows[half, e, pl.ds(pl.multiple_of(q * height, height), height), :] = picked[
                e * height:(e + 1) * height
            ]

    quads = RING // QUAD

    def gather_some(half, first, last):
        def body(step, carry):
            turn = lax.div(step, quads)
            group = rem(y + jnp.where(turn == 3, 2, jnp.where(turn == 2, -1, turn)), NY)
            gather(half, group * quads + lax.rem(step, quads))
            return carry

        lax.fori_loop(first, last, body, 0)

    def way(i):
        past = jnp.maximum(i - 2, 0)
        distance = jnp.where(i < 2, 0, lax.div(past, 4) + 1)
        side = lax.rem(past, 2)
        core = jnp.where(jnp.logical_or(i < 2, i == RING - 1), lax.rem(i, 2), lax.div(lax.rem(past, 4), 2))
        return distance, side, core

    def place(i):
        distance, side, core = way(i)
        return 2 * rem(jnp.where(side == 0, z + distance, z - distance + NZ), NZ) + core

    def unit(u):
        early = u < 2 * FIRST
        i = jnp.where(early, lax.rem(u, FIRST), lax.div(u, 2))
        half = jnp.where(early, lax.div(u, FIRST), lax.rem(u, 2))
        return i, half

    def load(i):
        slot = lax.rem(i, FIRST)
        return pltpu.make_async_copy(gbuf.at[place(i)], gv.at[slot], gl.at[slot])

    def bring(i):
        distance, side, core = way(i)
        index = place(i)
        size = SLOTS // 2

        @pl.when(distance < NZ // 2)
        def _():
            j = 2 * distance - 1 + side
            ref = gbuf.at[index, pl.ds((1 - c) * size, size)]
            rdma(ref, ref, ss.at[j, core], sr.at[j, core], x, sibling).wait_recv()

        @pl.when(distance == NZ // 2)
        def _():
            for j in (7, 8):
                ref = gbuf.at[index, pl.ds((1 - c) * size + (j % 2) * (size // 2), size // 2)]
                rdma(ref, ref, ss.at[j, core], sr.at[j, core], x, sibling).wait_recv()

        load(i).start()

    mid = PART // 2
    top, bottom = pl.ds(0, mid), pl.ds(mid, mid)
    opposite = rem(x + 2, NX)

    def first_copies(u):
        slot = lax.rem(u, DEPTH)
        return (
            rdma(part.at[slot, opposite, top], r1.at[u, 0], s1s.at[u, 0], s1r.at[u, 0], up_x, me),
            rdma(part.at[slot, opposite, bottom], r1.at[u, 1], s1s.at[u, 1], s1r.at[u, 1], down_x, me),
        )

    def second_copies(u):
        slot = lax.rem(u, DEPTH)
        return (
            rdma(part.at[slot, up_x], r2.at[u, 0], s2s.at[u, 0], s2r.at[u, 0], up_x, me),
            rdma(part.at[slot, down_x], r2.at[u, 1], s2s.at[u, 1], s2r.at[u, 1], down_x, me),
        )

    def sent(u):
        for copy in first_copies(u):
            copy.wait_send()
        for copy in second_copies(u):
            copy.wait_send()

    def out_copies(u, remote, local):
        i, half = unit(u)
        slot = lax.rem(u, KEEP)
        for k in range(NY // HALVES):
            target = half * (NY // HALVES) + k
            away = rem(target - y, NY)

            @pl.when(away != 0)
            def _():
                remote(rdma(
                    total.at[slot, k], out.at[y * RING + place(i)],
                    cs.at[slot, k], cr.at[i, away], x, target * RING + zc,
                ))

            @pl.when(away == 0)
            def _():
                local(pltpu.make_async_copy(total.at[slot, k], out.at[y * RING + place(i)], cl.at[slot]))

    def give(u):
        out_copies(u, lambda copy: copy.start(), lambda copy: copy.start())

    def given(u):
        out_copies(u, lambda copy: copy.wait_send(), lambda copy: copy.wait())

    def multiply(u):
        i, half = unit(u)
        slot, held = lax.rem(u, DEPTH), lax.rem(i, FIRST)
        expert = place(i)

        @pl.when(u >= DEPTH)
        def _():
            sent(u - DEPTH)

        @pl.when(jnp.logical_or(u < FIRST, jnp.logical_and(u >= 2 * FIRST, lax.rem(u, 2) == 0)))
        def _():
            pltpu.make_async_copy(grad.at[0], gv.at[held], gl.at[held]).wait()

        for t in range(NX):
            part[slot, t] = lax.dot_general(
                rows[half, expert], gv[held, :, t * HSH:(t + 1) * HSH],
                (((0,), (0,)), ((), ())), preferred_element_type=F32,
            ).astype(BF16)
        for copy in first_copies(u):
            copy.start()

    def combine(u):
        slot = lax.rem(u, DEPTH)
        for copy in first_copies(u):
            copy.wait_recv()
        part[slot, up_x, top] = (
            part[slot, up_x, top].astype(F32) + r1[u, 0].astype(F32)
        ).astype(BF16)
        part[slot, down_x, bottom] = (
            part[slot, down_x, bottom].astype(F32) + r1[u, 1].astype(F32)
        ).astype(BF16)
        for copy in second_copies(u):
            copy.start()

    def finish(u):
        slot = lax.rem(u, DEPTH)

        @pl.when(u >= KEEP)
        def _():
            given(u - KEEP)

        for copy in second_copies(u):
            copy.wait_recv()
        for k in range(NY // HALVES):
            span = pl.ds(k * COLS, COLS)
            total[lax.rem(u, KEEP), k] = (
                part[slot, x, span].astype(F32)
                + r2[u, 0, span].astype(F32)
                + r2[u, 1, span].astype(F32)
            ).astype(BF16)
        give(u)

    def repeat(function, first):
        def body(u, carry):
            function(u)
            return carry

        lax.fori_loop(first, first + 2, body, 0)

    def far_y_arrived(half):
        for j in range(NZ):
            far_copy(half, j, far_y).wait_recv()

    spread_y(0, 0, NZ)
    for h in range(2):
        others_rows(h).wait_recv()
    for core in range(2):
        @pl.when(c == core)
        def _():
            pltpu.make_async_copy(grad.at[0], gv.at[core], gl.at[core]).start()

        @pl.when(c != core)
        def _():
            load(jnp.int32(core)).start()

    issue(0)
    issue(1)
    gather_some(0, 0, quads)
    pass_y(0, 0, NZ)
    gather_some(0, quads, 3 * quads)
    spread_y(1, 0, NZ // 2)
    far_y_arrived(0)
    gather_some(0, 3 * quads, 4 * quads)
    repeat(multiply, 0)
    spread_y(1, NZ // 2, NZ)
    repeat(combine, 0)
    pass_y(1, 0, NZ // 2)
    repeat(finish, 0)
    gather_some(1, 0, quads)
    arrive(0)
    issue(2)
    bring(jnp.int32(2))
    bring(jnp.int32(3))
    repeat(multiply, 2)
    pass_y(1, NZ // 2, NZ)
    repeat(combine, 2)
    gather_some(1, quads, 3 * quads)
    far_y_arrived(1)
    gather_some(1, 3 * quads, 4 * quads)
    repeat(finish, 2)

    def close(i, carry):
        for k in range(1, NY):
            source = rem(y - k, NY)
            rdma(
                total.at[0, 0], out.at[source * RING + place(i)],
                cs.at[0, 0], cr.at[i, k], x, source * RING + zc,
            ).wait_recv()
        return carry

    def tokens_sent():
        for half in range(HALVES):
            for k in range(1, RING):
                z_copy(half, k, rem(zc + k, RING), zc).wait_send()
            for j in range(NZ):
                y_copy(half, 0, j, y, up_y).wait_send()
                y_copy(half, 1, j, y, down_y).wait_send()
                far_copy(half, j, up_y if j % 2 else down_y).wait_send()

    def shards_sent():
        for k in range(2):
            own_rows(k).wait_send()
            for j in range(1, 9):
                ring_copy(j, k, z).wait_send()
                pair_copy(j, k, c).wait_send()

    def main_step(u, carry):
        @pl.when(u < UNITS)
        def _():
            multiply(u)

        @pl.when(jnp.logical_and(u >= FIRST + 2, u < UNITS + 2))
        def _():
            combine(u - 2)

        @pl.when(u == 2 * RING - 20)
        def _():
            tokens_sent()

        @pl.when(u == UNITS + 1)
        def _():
            shards_sent()
            lax.fori_loop(0, RING - 3, close, 0)

        @pl.when(u >= FIRST + 4)
        def _():
            finish(u - 4)

        for n, at in ((1, 7), (2, 11), (3, 15), (4, 19), (5, 23), (6, 27), (7, 29)):
            @pl.when(u == at)
            def _():
                arrive(n)
                if n + 2 < NZ:
                    issue(n + 2)

        following = lax.div(u, 2) + 1
        odd = jnp.logical_and(lax.rem(following, 2) == 1, following < RING - 1)
        due = jnp.where(odd, lax.rem(u, 2) == 0, lax.rem(u, 2) == 1)

        @pl.when(jnp.logical_and(due, jnp.logical_and(following >= FIRST, following < RING)))
        def _():
            bring(following)

        return carry

    lax.fori_loop(FIRST, UNITS + 4, main_step, 0)

    lax.fori_loop(RING - 3, RING, close, 0)

    def close_units(u, carry):
        sent(u)
        return carry

    def close_outs(u, carry):
        given(u)
        return carry

    lax.fori_loop(UNITS - DEPTH, UNITS, close_units, 0)
    lax.fori_loop(UNITS - KEEP, UNITS, close_outs, 0)


def local(stash_codes, stash_scales, expert_ids, grad_rows):
    vmem = pl.BlockSpec(memory_space=pltpu.VMEM)
    hbm = pl.BlockSpec(memory_space=pl.ANY)
    dma = pltpu.SemaphoreType.DMA
    weight_grad, _ = pl.pallas_call(
        kernel,
        out_shape=(
            pltpu.VMEM((OWNERS, COLS, HSH), BF16),
            jax.ShapeDtypeStruct((RING, SLOTS, HW), BF16),
        ),
        in_specs=[hbm, vmem, vmem, hbm],
        out_specs=(vmem, hbm),
        scratch_shapes=[
            pltpu.VMEM((TOK, D), BF16),
            pltpu.VMEM((RING, PART + TAB, TOK), BF16),
            pltpu.VMEM((RING, PART, TOK), BF16),
            pltpu.VMEM((OWNERS, PART + TAB, TOK), BF16),
            pltpu.VMEM((OWNERS, PART, TOK), BF16),
            pltpu.VMEM((OWNERS // QUAD, QUAD * RING, TOK), F32),
            pltpu.VMEM((RING * QUAD * CAP, QUAD * TOK), BF16),
            pltpu.VMEM((HALVES, RING, SLOTS, PART), BF16),
            pltpu.VMEM((FIRST, SLOTS, HW), BF16),
            pltpu.VMEM((DEPTH, NX, PART, HSH), BF16),
            pltpu.VMEM((UNITS, 2, PART // 2, HSH), BF16),
            pltpu.VMEM((UNITS, 2, PART, HSH), BF16),
            pltpu.VMEM((KEEP, NY // HALVES, COLS, HSH), BF16),
            dma((CUTS,)), dma((HALVES,)),
            dma((HALVES, RING)), dma((HALVES, RING)),
            dma((HALVES, 2, NZ)), dma((HALVES, 2, NZ)), dma((HALVES, NZ)), dma((HALVES, NZ)),
            dma((9, 2)), dma((9, 2)), dma((9, 2)), dma((9, 2)), dma((FIRST,)),
            dma((UNITS, 2)), dma((UNITS, 2)), dma((UNITS, 2)), dma((UNITS, 2)),
            dma((KEEP, 2)), dma((RING, NY)), dma((KEEP,)),
        ],
        compiler_params=pltpu.CompilerParams(
            collective_id=0, has_side_effects=True, vmem_limit_bytes=56 * 1024 * 1024
        ),
        cost_estimate=pl.CostEstimate(
            flops=2 * SLOTS * D * HW, bytes_accessed=100_000_000, transcendentals=0
        ),
    )(stash_codes, stash_scales.T, expert_ids.T, grad_rows)
    return weight_grad


def solution(mesh):
    return jax.shard_map(
        local,
        mesh=mesh,
        in_specs=(
            P(("dp", "expert"), None),
            P(("dp", "expert"), None),
            P(("dp", "expert"), None),
            P(("dp", "expert"), None, None),
        ),
        out_specs=P(None, "expert", "dp"),
        check_vma=False,
    )
```

```python
import jax
import jax.numpy as jnp
from jax import lax
from jax.experimental import pallas as pl
from jax.experimental.pallas import tpu as pltpu
from jax.sharding import PartitionSpec as P

QB = 128
EXP_DEV = 4
CAP = 12
D = 7168
HW = 1024
TOK = 128
NX, NY, NZ = 4, 4, 8
RING = 2 * NZ
OWNERS = NY * RING
COLS = D // OWNERS
WIDTH = NY * COLS
SLOTS = OWNERS * CAP
HSH = HW // NX
TOPK = 8
TAB = 16
HALVES = 2
PART = WIDTH // HALVES
UNITS = RING * HALVES
FIRST = 4
DEPTH = 6
KEEP = 4
CUTS = 4
QUAD = 4
MESH = pl.DeviceIdType.MESH
BF16 = jnp.bfloat16
F32 = jnp.float32


def rem(value, count):
    return lax.rem(value + count, count)


def kernel(
    codes, scales, ids, grad, out, gbuf,
    code, send0, send1, tok0, tok1, ranks, onehot, rows, gv, part, r1, r2, total,
    il, ol, zs, zr, ys, yr, yfs, yfr, gs, gr, ss, sr, gl,
    s1s, s1r, s2s, s2r, cs, cr, cl,
):
    x = lax.axis_index("dp")
    me = lax.axis_index("expert")
    y = lax.div(me, RING)
    zc = lax.rem(me, RING)
    z = lax.div(zc, 2)
    c = lax.rem(zc, 2)
    own = zc
    up_x, down_x = rem(x + 1, NX), rem(x - 1, NX)
    up_y, down_y = rem(y + 1, NY), rem(y - 1, NY)
    far_y = rem(y + 2, NY)
    dev_up_z = y * RING + 2 * rem(z + 1, NZ) + c
    dev_down_z = y * RING + 2 * rem(z - 1, NZ) + c
    sibling = y * RING + 2 * z + (1 - c)
    send, tok = (send0, send1), (tok0, tok1)

    def rdma(src, dst, send_sem, recv_sem, dev_x, dev_e):
        return pltpu.make_async_remote_copy(
            src_ref=src, dst_ref=dst, send_sem=send_sem, recv_sem=recv_sem,
            device_id=(dev_x, dev_e), device_id_type=MESH,
        )

    step = D // CUTS
    fetches = [
        pltpu.make_async_copy(
            codes.at[:, pl.ds(k * step, step)], code.at[:, pl.ds(k * step, step)], il.at[k]
        )
        for k in range(CUTS)
    ]
    for fetch in fetches:
        fetch.start()

    barrier = pltpu.get_barrier_semaphore()
    for k in range(1, RING):
        pl.semaphore_signal(barrier, inc=1, device_id=(x, y * RING + rem(zc + k, RING)), device_id_type=MESH)
    for k in range(1, NY):
        pl.semaphore_signal(barrier, inc=1, device_id=(x, rem(y + k, NY) * RING + zc), device_id_type=MESH)
    for dev_x in (up_x, down_x):
        pl.semaphore_signal(barrier, inc=1, device_id=(dev_x, me), device_id_type=MESH)

    row_id = lax.broadcasted_iota(jnp.int32, (QB, QB), 0)
    col_id = lax.broadcasted_iota(jnp.int32, (QB, QB), 1)
    common = row_id & col_id
    parity = jnp.zeros((QB, QB), jnp.int32)
    for bit in range(7):
        parity = parity + ((common >> bit) & 1)
    had = (1 - 2 * (parity & 1)).astype(F32).astype(BF16)

    def restore(half):
        blocks = D // QB // HALVES
        for k in range(half * blocks, (half + 1) * blocks):
            if k % (D // QB // CUTS) == 0:
                fetches[k // (D // QB // CUTS)].wait()
            turned = lax.dot_general(
                had, code[:, k * QB:(k + 1) * QB], (((1,), (1,)), ((), ())), preferred_element_type=F32
            )
            turned = (turned * (scales[k:k + 1, :] * QB ** (-0.5))).astype(BF16)
            start = 0
            while start < QB:
                n = k * QB + start
                idx, off = n // COLS, n % COLS
                length = min(QB - start, COLS - off)
                ty, tz = idx // RING, idx % RING
                at = (ty - half * (NY // HALVES)) * COLS + off
                send[half][tz, at:at + length, :] = turned[start:start + length]
                start += length

    def z_copy(half, k, target, source):
        return rdma(
            send[half].at[target], tok[half].at[y * RING + source],
            zs.at[half, k], zr.at[half, k], x, y * RING + target,
        )

    own_copies = [
        pltpu.make_async_copy(send[half].at[own], tok[half].at[me], ol.at[half]) for half in range(HALVES)
    ]

    def z_group(half, distance):
        for chip in ([z] if distance == 0 else [z + distance, z - distance][:1 if distance == NZ // 2 else 2]):
            for core in ([1 - c] if distance == 0 else [0, 1]):
                target = 2 * rem(chip, NZ) + core
                z_copy(half, rem(target - zc, RING), target, zc).start()

    named = jnp.concatenate(
        [ids[...].astype(F32), jnp.zeros((TAB - TOPK, TOK), F32)], axis=0
    ).astype(BF16)
    for k in range(RING):
        send0[k, PART:PART + TAB, :] = named
    def own_rows(h):
        span = pl.ds(h * (SLOTS // 2), SLOTS // 2)
        return rdma(grad.at[0, span], gbuf.at[own, span], ss.at[0, h], sr.at[0, h], x, sibling)

    for half in range(HALVES):
        restore(half)
        if half == 0:
            pl.semaphore_wait(barrier, RING - 1 + NY - 1 + 2)
        for distance in range(NZ // 2 + 1):
            z_group(half, distance)
        own_copies[half].start()
        if half == 0:
            for h in range(2):
                own_rows(h).start()

    def ring_z(j):
        return rem(z + (j + 1) // 2, NZ) if j % 2 else rem(z - j // 2, NZ)

    def cut(index, core, j):
        size = SLOTS // 2
        if j < 7:
            return gbuf.at[index, pl.ds(core * size, size)]
        return gbuf.at[index, pl.ds(core * size + (j % 2) * (size // 2), size // 2)]

    def ring_copy(j, k, source):
        ref = cut(2 * source + k, c, j)
        return rdma(ref, ref, gs.at[j, k], gr.at[j, k], x, dev_down_z if j % 2 else dev_up_z)

    def pair_copy(j, k, core):
        ref = cut(2 * ring_z(j) + k, core, j)
        return rdma(ref, ref, ss.at[j, k], sr.at[j, k], x, sibling)

    def others_rows(h):
        span = pl.ds(h * (SLOTS // 2), SLOTS // 2)
        index = 2 * z + (1 - c)
        return rdma(gbuf.at[index, span], gbuf.at[index, span], ss.at[0, h], sr.at[0, h], x, sibling)

    def own_copy(j):
        span = pl.ds(c * (SLOTS // 2), SLOTS // 2)
        return rdma(
            grad.at[0, span], gbuf.at[own, span], gs.at[j, c], gr.at[j, c],
            x, dev_down_z if j % 2 else dev_up_z,
        )

    def issue(n):
        distance, k = n // 2, n % 2
        for j in (2 * distance - 1, 2 * distance):
            if n >= 2:
                ring_copy(j + 2, k, ring_z(j)).start()
                continue

            @pl.when(c == k)
            def _():
                own_copy(j + 2).start()

            @pl.when(c != k)
            def _():
                ring_copy(j + 2, k, z).start()

    def arrive(n):
        distance, k = n // 2 + 1, n % 2
        for j in (2 * distance - 1, 2 * distance):
            ring_copy(j, k, ring_z(j)).wait_recv()
            pair_copy(j, k, c).start()

    def chunk(half, group, j):
        return tok[half].at[pl.ds(group * RING + 2 * ring_z(j), 2)]

    def y_copy(half, way, j, group, target):
        ref = chunk(half, group, j)
        return rdma(ref, ref, ys.at[half, way, j], yr.at[half, way, j], x, target * RING + zc)

    def far_copy(half, j, group):
        ref = chunk(half, group, j)
        target = down_y if j % 2 else up_y
        return rdma(ref, ref, yfs.at[half, j], yfr.at[half, j], x, target * RING + zc)

    def spread_y(half, first, last):
        for j in range(first, last):
            if j == 0:
                own_copies[half].wait()
            for source in ([2 * z + (1 - c)] if j == 0 else [2 * ring_z(j), 2 * ring_z(j) + 1]):
                z_copy(half, rem(zc - source, RING), source, source).wait_recv()
            y_copy(half, 0, j, y, up_y).start()
            y_copy(half, 1, j, y, down_y).start()

    def pass_y(half, first, last):
        for j in range(first, last):
            y_copy(half, 0, j, down_y, up_y).wait_recv()
            y_copy(half, 1, j, up_y, down_y).wait_recv()
            far_copy(half, j, up_y if j % 2 else down_y).start()

    before = jnp.where(
        lax.broadcasted_iota(jnp.int32, (TOK, TOK), 0) < lax.broadcasted_iota(jnp.int32, (TOK, TOK), 1),
        1.0, 0.0,
    ).astype(BF16)
    expert_id = (lax.broadcasted_iota(jnp.int32, (RING, TOK), 0) * EXP_DEV + y * (RING * EXP_DEV)).astype(F32)
    slot_row = lax.broadcasted_iota(jnp.int32, (QUAD * CAP, TOK), 0).astype(F32)

    def rank(q):
        members = []
        for p in range(QUAD):
            words = tok0[QUAD * q + p, PART:PART + TAB, :].astype(F32)
            member = jnp.zeros((RING, TOK), F32)
            for k in range(TOPK):
                member = jnp.where(expert_id == words[k:k + 1, :], 1.0, member)
            members.append(member)
        member = jnp.concatenate(members, axis=0)
        order = lax.dot_general(
            member.astype(BF16), before, (((1,), (0,)), ((), ())), preferred_element_type=F32
        )
        ranks[q] = jnp.where(member > 0.5, order, -100.0)

    def gather(half, q):
        if half == 0:
            rank(q)
        height = QUAD * CAP
        for p in range(QUAD):
            for e in range(RING):
                taken = ranks[q, p * RING + e:p * RING + e + 1, :]
                onehot[e * height:(e + 1) * height, p * TOK:(p + 1) * TOK] = jnp.where(
                    taken == slot_row - p * CAP, 1.0, 0.0
                ).astype(BF16)
        blocks = jnp.concatenate([tok[half][QUAD * q + p, 0:PART, :] for p in range(QUAD)], axis=1)
        picked = lax.dot_general(
            onehot[...], blocks, (((1,), (1,)), ((), ())), preferred_element_type=F32
        ).astype(BF16)
        for e in range(RING):
            rows[half, e, pl.ds(pl.multiple_of(q * height, height), height), :] = picked[
                e * height:(e + 1) * height
            ]

    quads = RING // QUAD

    def gather_some(half, first, last):
        def body(step, carry):
            turn = lax.div(step, quads)
            group = rem(y + jnp.where(turn == 3, 2, jnp.where(turn == 2, -1, turn)), NY)
            gather(half, group * quads + lax.rem(step, quads))
            return carry

        lax.fori_loop(first, last, body, 0)

    def way(i):
        past = jnp.maximum(i - 2, 0)
        distance = jnp.where(i < 2, 0, lax.div(past, 4) + 1)
        side = lax.rem(past, 2)
        core = jnp.where(jnp.logical_or(i < 2, i == RING - 1), lax.rem(i, 2), lax.div(lax.rem(past, 4), 2))
        return distance, side, core

    def place(i):
        distance, side, core = way(i)
        return 2 * rem(jnp.where(side == 0, z + distance, z - distance + NZ), NZ) + core

    def unit(u):
        early = u < 2 * FIRST
        i = jnp.where(early, lax.rem(u, FIRST), lax.div(u, 2))
        half = jnp.where(early, lax.div(u, FIRST), lax.rem(u, 2))
        return i, half

    def load(i):
        slot = lax.rem(i, FIRST)
        return pltpu.make_async_copy(gbuf.at[place(i)], gv.at[slot], gl.at[slot])

    def bring(i):
        distance, side, core = way(i)
        index = place(i)
        size = SLOTS // 2

        @pl.when(distance < NZ // 2)
        def _():
            j = 2 * distance - 1 + side
            ref = gbuf.at[index, pl.ds((1 - c) * size, size)]
            rdma(ref, ref, ss.at[j, core], sr.at[j, core], x, sibling).wait_recv()

        @pl.when(distance == NZ // 2)
        def _():
            for j in (7, 8):
                ref = gbuf.at[index, pl.ds((1 - c) * size + (j % 2) * (size // 2), size // 2)]
                rdma(ref, ref, ss.at[j, core], sr.at[j, core], x, sibling).wait_recv()

        load(i).start()

    mid = PART // 2
    top, bottom = pl.ds(0, mid), pl.ds(mid, mid)
    opposite = rem(x + 2, NX)

    def first_copies(u):
        slot = lax.rem(u, DEPTH)
        return (
            rdma(part.at[slot, opposite, top], r1.at[u, 0], s1s.at[u, 0], s1r.at[u, 0], up_x, me),
            rdma(part.at[slot, opposite, bottom], r1.at[u, 1], s1s.at[u, 1], s1r.at[u, 1], down_x, me),
        )

    def second_copies(u):
        slot = lax.rem(u, DEPTH)
        return (
            rdma(part.at[slot, up_x], r2.at[u, 0], s2s.at[u, 0], s2r.at[u, 0], up_x, me),
            rdma(part.at[slot, down_x], r2.at[u, 1], s2s.at[u, 1], s2r.at[u, 1], down_x, me),
        )

    def sent(u):
        for copy in first_copies(u):
            copy.wait_send()
        for copy in second_copies(u):
            copy.wait_send()

    def out_copies(u, remote, local):
        i, half = unit(u)
        slot = lax.rem(u, KEEP)
        for k in range(NY // HALVES):
            target = half * (NY // HALVES) + k
            away = rem(target - y, NY)

            @pl.when(away != 0)
            def _():
                remote(rdma(
                    total.at[slot, k], out.at[y * RING + place(i)],
                    cs.at[slot, k], cr.at[i, away], x, target * RING + zc,
                ))

            @pl.when(away == 0)
            def _():
                local(pltpu.make_async_copy(total.at[slot, k], out.at[y * RING + place(i)], cl.at[slot]))

    def give(u):
        out_copies(u, lambda copy: copy.start(), lambda copy: copy.start())

    def given(u):
        out_copies(u, lambda copy: copy.wait_send(), lambda copy: copy.wait())

    def multiply(u):
        i, half = unit(u)
        slot, held = lax.rem(u, DEPTH), lax.rem(i, FIRST)
        expert = place(i)

        @pl.when(u >= DEPTH)
        def _():
            sent(u - DEPTH)

        @pl.when(jnp.logical_or(u < FIRST, jnp.logical_and(u >= 2 * FIRST, lax.rem(u, 2) == 0)))
        def _():
            pltpu.make_async_copy(grad.at[0], gv.at[held], gl.at[held]).wait()

        for t in range(NX):
            part[slot, t] = lax.dot_general(
                rows[half, expert], gv[held, :, t * HSH:(t + 1) * HSH],
                (((0,), (0,)), ((), ())), preferred_element_type=F32,
            ).astype(BF16)
        for copy in first_copies(u):
            copy.start()

    def combine(u):
        slot = lax.rem(u, DEPTH)
        for copy in first_copies(u):
            copy.wait_recv()
        part[slot, up_x, top] = (
            part[slot, up_x, top].astype(F32) + r1[u, 0].astype(F32)
        ).astype(BF16)
        part[slot, down_x, bottom] = (
            part[slot, down_x, bottom].astype(F32) + r1[u, 1].astype(F32)
        ).astype(BF16)
        for copy in second_copies(u):
            copy.start()

    def finish(u):
        slot = lax.rem(u, DEPTH)

        @pl.when(u >= KEEP)
        def _():
            given(u - KEEP)

        for copy in second_copies(u):
            copy.wait_recv()
        for k in range(NY // HALVES):
            span = pl.ds(k * COLS, COLS)
            total[lax.rem(u, KEEP), k] = (
                part[slot, x, span].astype(F32)
                + r2[u, 0, span].astype(F32)
                + r2[u, 1, span].astype(F32)
            ).astype(BF16)
        give(u)

    def repeat(function, first):
        def body(u, carry):
            function(u)
            return carry

        lax.fori_loop(first, first + 2, body, 0)

    def far_y_arrived(half):
        for j in range(NZ):
            far_copy(half, j, far_y).wait_recv()

    spread_y(0, 0, NZ)
    for h in range(2):
        others_rows(h).wait_recv()
    for core in range(2):
        @pl.when(c == core)
        def _():
            pltpu.make_async_copy(grad.at[0], gv.at[core], gl.at[core]).start()

        @pl.when(c != core)
        def _():
            load(jnp.int32(core)).start()

    issue(0)
    issue(1)
    gather_some(0, 0, quads)
    pass_y(0, 0, NZ)
    gather_some(0, quads, 3 * quads)
    spread_y(1, 0, NZ // 2)
    far_y_arrived(0)
    gather_some(0, 3 * quads, 4 * quads)
    repeat(multiply, 0)
    spread_y(1, NZ // 2, NZ)
    repeat(combine, 0)
    pass_y(1, 0, NZ // 2)
    repeat(finish, 0)
    gather_some(1, 0, quads)
    arrive(0)
    issue(2)
    bring(jnp.int32(2))
    bring(jnp.int32(3))
    repeat(multiply, 2)
    pass_y(1, NZ // 2, NZ)
    repeat(combine, 2)
    gather_some(1, quads, 3 * quads)
    far_y_arrived(1)
    gather_some(1, 3 * quads, 4 * quads)
    repeat(finish, 2)

    def close(i, carry):
        for k in range(1, NY):
            source = rem(y - k, NY)
            rdma(
                total.at[0, 0], out.at[source * RING + place(i)],
                cs.at[0, 0], cr.at[i, k], x, source * RING + zc,
            ).wait_recv()
        return carry

    def tokens_sent():
        for half in range(HALVES):
            for k in range(1, RING):
                z_copy(half, k, rem(zc + k, RING), zc).wait_send()
            for j in range(NZ):
                y_copy(half, 0, j, y, up_y).wait_send()
                y_copy(half, 1, j, y, down_y).wait_send()
                far_copy(half, j, up_y if j % 2 else down_y).wait_send()

    def shards_sent():
        for k in range(2):
            own_rows(k).wait_send()
            for j in range(1, 9):
                ring_copy(j, k, z).wait_send()
                pair_copy(j, k, c).wait_send()

    def main_step(u, carry):
        @pl.when(jnp.logical_and(u >= FIRST + 2, u < UNITS + 2))
        def _():
            combine(u - 2)

        @pl.when(u < UNITS)
        def _():
            multiply(u)

        @pl.when(u == 2 * RING - 20)
        def _():
            tokens_sent()

        @pl.when(u == UNITS + 1)
        def _():
            shards_sent()
            lax.fori_loop(0, RING - 3, close, 0)

        @pl.when(u >= FIRST + 4)
        def _():
            finish(u - 4)

        for n, at in ((1, 7), (2, 11), (3, 15), (4, 19), (5, 23), (6, 27), (7, 29)):
            @pl.when(u == at)
            def _():
                arrive(n)
                if n + 2 < NZ:
                    issue(n + 2)

        following = lax.div(u, 2) + 1
        odd = jnp.logical_and(lax.rem(following, 2) == 1, following < RING - 1)
        due = jnp.where(odd, lax.rem(u, 2) == 0, lax.rem(u, 2) == 1)

        @pl.when(jnp.logical_and(due, jnp.logical_and(following >= FIRST, following < RING)))
        def _():
            bring(following)

        return carry

    lax.fori_loop(FIRST, UNITS + 4, main_step, 0)

    lax.fori_loop(RING - 3, RING, close, 0)

    def close_units(u, carry):
        sent(u)
        return carry

    def close_outs(u, carry):
        given(u)
        return carry

    lax.fori_loop(UNITS - DEPTH, UNITS, close_units, 0)
    lax.fori_loop(UNITS - KEEP, UNITS, close_outs, 0)


def local(stash_codes, stash_scales, expert_ids, grad_rows):
    vmem = pl.BlockSpec(memory_space=pltpu.VMEM)
    hbm = pl.BlockSpec(memory_space=pl.ANY)
    dma = pltpu.SemaphoreType.DMA
    weight_grad, _ = pl.pallas_call(
        kernel,
        out_shape=(
            pltpu.VMEM((OWNERS, COLS, HSH), BF16),
            jax.ShapeDtypeStruct((RING, SLOTS, HW), BF16),
        ),
        in_specs=[hbm, vmem, vmem, hbm],
        out_specs=(vmem, hbm),
        scratch_shapes=[
            pltpu.VMEM((TOK, D), BF16),
            pltpu.VMEM((RING, PART + TAB, TOK), BF16),
            pltpu.VMEM((RING, PART, TOK), BF16),
            pltpu.VMEM((OWNERS, PART + TAB, TOK), BF16),
            pltpu.VMEM((OWNERS, PART, TOK), BF16),
            pltpu.VMEM((OWNERS // QUAD, QUAD * RING, TOK), F32),
            pltpu.VMEM((RING * QUAD * CAP, QUAD * TOK), BF16),
            pltpu.VMEM((HALVES, RING, SLOTS, PART), BF16),
            pltpu.VMEM((FIRST, SLOTS, HW), BF16),
            pltpu.VMEM((DEPTH, NX, PART, HSH), BF16),
            pltpu.VMEM((UNITS, 2, PART // 2, HSH), BF16),
            pltpu.VMEM((UNITS, 2, PART, HSH), BF16),
            pltpu.VMEM((KEEP, NY // HALVES, COLS, HSH), BF16),
            dma((CUTS,)), dma((HALVES,)),
            dma((HALVES, RING)), dma((HALVES, RING)),
            dma((HALVES, 2, NZ)), dma((HALVES, 2, NZ)), dma((HALVES, NZ)), dma((HALVES, NZ)),
            dma((9, 2)), dma((9, 2)), dma((9, 2)), dma((9, 2)), dma((FIRST,)),
            dma((UNITS, 2)), dma((UNITS, 2)), dma((UNITS, 2)), dma((UNITS, 2)),
            dma((KEEP, 2)), dma((RING, NY)), dma((KEEP,)),
        ],
        compiler_params=pltpu.CompilerParams(
            collective_id=0, has_side_effects=True, vmem_limit_bytes=56 * 1024 * 1024
        ),
        cost_estimate=pl.CostEstimate(
            flops=2 * SLOTS * D * HW, bytes_accessed=100_000_000, transcendentals=0
        ),
    )(stash_codes, stash_scales.T, expert_ids.T, grad_rows)
    return weight_grad


def solution(mesh):
    return jax.shard_map(
        local,
        mesh=mesh,
        in_specs=(
            P(("dp", "expert"), None),
            P(("dp", "expert"), None),
            P(("dp", "expert"), None),
            P(("dp", "expert"), None, None),
        ),
        out_specs=P(None, "expert", "dp"),
        check_vma=False,
    )
```
